256 devices in a mesh: dp: 64 (over z, y, core), mp: 4 (over x).
Axes of the slice: x: 4, y: 4, z: 8, core: 2. Of those that a mesh axis runs over, the one named last changes fastest.
Arguments:
- activations: bfloat16 [32768, 3072], P('dp', 'mp'), may hold values from -16 to 16
- cotangent: bfloat16 [32768, 6144], P('dp', 'mp'), may hold values from -6 to 6
- block_owner: int32 [72], replicated, may hold values from 0 to 63, as said below
- left_factor: float32 [128, 1024, 256], P('dp', 'mp'), as said below
- right_factor: float32 [128, 1024, 256], P('dp', 'mp'), as said below
- left_basis: float32 [128, 1024, 256], P('dp', 'mp')
- right_basis: float32 [128, 1024, 256], P('dp', 'mp')
Outputs:
- update: bfloat16 [256, 12, 6144], P('dp', None, 'mp')
- left_next: float32 [128, 1024, 256], P('dp', 'mp')
- right_next: float32 [128, 1024, 256], P('dp', 'mp')
- left_basis_next: float32 [128, 1024, 256], P('dp', 'mp')
- right_basis_next: float32 [128, 1024, 256], P('dp', 'mp')
The draws below stay inside these ranges and needn't reach their ends.
Inputs may be any that keep to these rules, and one draw needn't show every extreme that they name: Block b is held by dp index block_owner[b]; every dp index holds 1 or 2 blocks, so at most 2. `left_factor`: every 256 x 256 block is symmetric positive definite. `right_factor`: every 256 x 256 block is symmetric positive definite.
All inputs are finite; a program needn't handle non-finite values.
Results may differ from the reference program's by a relative error of at most 0.001.
Values may be sent and summed in bfloat16 or wider, within the bound.
A program may use at most 256 MiB of HBM per device.

```python
import math
import jax
import jax.numpy as jnp
from jax import lax

BS = 256
IN_ROWS = 3072
COLS = 6144
NSTEPS = 6
TOKENS = 32768
BANDS = 12
NBLK = 72
CAP = 2
N_DP = 64
N_MP = 4


def definite_blocks(key, count, order_size, top, lower, width):
    key_rows, key_off, key_diag = jax.random.split(key, 3)
    spread = jnp.exp(jax.random.uniform(key_rows, (count, order_size), minval=0.0, maxval=math.log(top)))
    noise = jax.random.uniform(key_off, (count, order_size, order_size), minval=-1.0, maxval=1.0)
    coupling = (noise + jnp.swapaxes(noise, 1, 2)) * (0.5 / (1.2 * order_size))
    identity = jnp.eye(order_size, dtype=jnp.float32)
    diagonal = lower + width * jax.random.uniform(key_diag, (count, order_size))
    core = coupling * (1.0 - identity) + identity * diagonal[:, :, None]
    root = jnp.sqrt(spread)
    return core * root[:, :, None] * root[:, None, :]


def draw_block_owner(key, part):
    key = jax.random.fold_in(key, 21)
    key_owner, key_block = jax.random.split(key)
    owners = jax.random.permutation(key_owner, N_DP)
    positions = jax.random.permutation(key_block, NBLK)
    return owners[positions % N_DP].astype(jnp.int32)


def draw_left_factor(key, part):
    key = jax.random.fold_in(key, 31)
    blocks = definite_blocks(key, N_DP * CAP * N_MP, BS, 10.0, 0.9, 0.4)
    return blocks.reshape(N_DP * CAP, N_MP * BS, BS)


def draw_right_factor(key, part):
    key = jax.random.fold_in(key, 41)
    blocks = definite_blocks(key, N_DP * CAP * N_MP, BS, 10.0, 0.9, 0.4)
    return blocks.reshape(N_DP * CAP, N_MP * BS, BS)


def draw_left_basis(key, part):
    key = jax.random.fold_in(key, 51)
    key_value, key_column = jax.random.split(key)
    shape = (N_DP * CAP * N_MP, BS, BS)
    values = jax.random.normal(key_value, shape)
    column_scale = jnp.exp(jax.random.uniform(key_column, (N_DP * CAP * N_MP, 1, BS), minval=math.log(0.5), maxval=math.log(2.0)))
    return (values * column_scale / math.sqrt(BS)).reshape(N_DP * CAP, N_MP * BS, BS)


def draw_right_basis(key, part):
    key = jax.random.fold_in(key, 61)
    key_value, key_column = jax.random.split(key)
    shape = (N_DP * CAP * N_MP, BS, BS)
    values = jax.random.normal(key_value, shape)
    column_scale = jnp.exp(jax.random.uniform(key_column, (N_DP * CAP * N_MP, 1, BS), minval=math.log(0.5), maxval=math.log(2.0)))
    return (values * column_scale / math.sqrt(BS)).reshape(N_DP * CAP, N_MP * BS, BS)


def raised(values, stream_key, source, target, shards_of, factor):
    owner, partner = [(jnp.arange(values.shape[dim]) // (values.shape[dim] // shards_of)).reshape([-1 if axis == dim else 1 for axis in range(values.ndim)]) for dim in (source, target)]
    chosen = jax.random.permutation(stream_key, shards_of)[partner]
    strong = (owner == chosen) | (owner == (partner + shards_of // 2) % shards_of)
    return jnp.where(strong, factor * values, values)


def block_levels(stream_key, dims, shards, least, largest):
    def one(position, blocks):
        draws = jax.random.uniform(jax.random.fold_in(jax.random.fold_in(stream_key, 6), position), (blocks,), jnp.float32, least / len(shards), largest / len(shards))
        return jnp.repeat(jnp.exp(draws), dims[position] // blocks).reshape((-1,) + (1,) * (len(dims) - position - 1))

    level = one(*shards[0])
    for cut in shards[1:]:
        level = level * one(*cut)
    return level


def scatter_about(stream_key, extent, scale, limit, cuts=(), held_as=jnp.bfloat16):
    drawn = scale * jax.random.normal(stream_key, extent, jnp.float32)
    if cuts:
        drawn = drawn * block_levels(stream_key, extent, cuts, -0.22, 0.18)
    return jnp.clip(drawn, -limit, limit).astype(held_as)


def heavy_noise(own_key, extent, scale, most, shards, heavy, held_as=jnp.bfloat16):
    values = scale * jax.random.normal(own_key, extent, jnp.float32)
    if shards:
        values = values * block_levels(own_key, extent, shards, -0.22, 0.18)
    return jnp.clip(raised(values, jax.random.fold_in(own_key, 3), *heavy), -most, most).astype(held_as)


def setup_inputs(seed: int = 0) -> dict:
    key_list = jax.random.split(jax.random.key(seed), 8)
    activations = heavy_noise(key_list[0], (TOKENS, IN_ROWS), 1.0, 16.0, ((0, 64), (1, 4)), (0, 1, 64, 4.0))
    cotangent = scatter_about(key_list[1], (TOKENS, COLS), 1.0, 6.0, ((0, 64), (1, 4)))
    block_owner = draw_block_owner(jax.random.fold_in(key_list[7], 71), 0)
    left_factor = draw_left_factor(jax.random.fold_in(key_list[7], 71), 0)
    right_factor = draw_right_factor(jax.random.fold_in(key_list[7], 71), 0)
    left_basis = draw_left_basis(jax.random.fold_in(key_list[7], 71), 0)
    right_basis = draw_right_basis(jax.random.fold_in(key_list[7], 71), 0)
    return {"activations": activations, "cotangent": cotangent, "block_owner": block_owner, "left_factor": left_factor, "right_factor": right_factor, "left_basis": left_basis, "right_basis": right_basis}


BETA = 0.9
EPS = 1e-06
HIGHEST = lax.Precision.HIGHEST

def product(left_side, right_side):
    return jnp.dot(left_side, right_side, precision=HIGHEST, preferred_element_type=jnp.float32)

def slot_numbers(block_owner, capacity):
    positions = jnp.arange(block_owner.shape[0], dtype=jnp.int32)
    same_owner = block_owner[:, None] == block_owner[None, :]
    earlier = positions[None, :] < positions[:, None]
    slot_rank = lax.optimization_barrier(jnp.sum(jnp.where(same_owner & earlier, 1, 0), axis=1)).astype(jnp.int32)
    return (block_owner * capacity + slot_rank).astype(jnp.int32)

def orthogonalize(matrix):
    current = matrix / jnp.sqrt(jnp.sum(matrix * matrix) + EPS)
    identity = jnp.eye(matrix.shape[0], dtype=jnp.float32)
    for _ in range(NSTEPS):
        current = product(current, 1.5 * identity - 0.5 * product(current.T, current))
    return current

def refresh(gradient, left_old, right_old, left_prev, right_prev):
    order_size = gradient.shape[0]
    left_new = BETA * left_old + (1.0 - BETA) / order_size * product(gradient, gradient.T)
    right_new = BETA * right_old + (1.0 - BETA) / order_size * product(gradient.T, gradient)
    left_power = product(left_new, left_prev)
    right_power = product(right_new, right_prev)
    left_fresh = orthogonalize(left_power)
    right_fresh = orthogonalize(right_power)
    left_scale = (lax.optimization_barrier(jnp.mean(left_power * left_power, axis=0)) + EPS) ** (-0.125)
    right_scale = (lax.optimization_barrier(jnp.mean(right_power * right_power, axis=0)) + EPS) ** (-0.125)
    rotated = product(product(left_fresh.T, gradient), right_fresh)
    rotated = rotated * left_scale[:, None] * right_scale[None, :]
    block_update = product(product(left_fresh, rotated), right_fresh.T).astype(jnp.bfloat16)
    return (block_update, left_new, right_new, left_fresh, right_fresh)

def reference(activations, cotangent, block_owner, left_factor, right_factor, left_basis, right_basis):
    gradient = jnp.dot(activations.T, cotangent, preferred_element_type=jnp.float32) * (1.0 / math.sqrt(TOKENS))
    slot_ids = slot_numbers(block_owner, CAP)
    col_width = COLS // N_MP
    col_blocks = col_width // BS
    left_out, right_out = (left_factor, right_factor)
    left_basis_out, right_basis_out = (left_basis, right_basis)
    pieces = []
    for mp_group in range(N_MP):
        columns = gradient[:, mp_group * col_width:(mp_group + 1) * col_width]
        blocks = columns.reshape(BANDS, BS, col_blocks, BS).transpose(0, 2, 1, 3).reshape(NBLK, BS, BS)
        row_slice = slice(mp_group * BS, (mp_group + 1) * BS)
        inputs = (blocks, left_factor[slot_ids, row_slice], right_factor[slot_ids, row_slice], left_basis[slot_ids, row_slice], right_basis[slot_ids, row_slice])
        block_updates, left_new, right_new, left_fresh, right_fresh = lax.map(lambda entries: refresh(*entries), inputs)
        pieces.append(block_updates.reshape(BANDS, col_blocks, BS, BS).transpose(2, 0, 1, 3).reshape(BS, BANDS, col_width))
        left_out = left_out.at[slot_ids, row_slice].set(left_new)
        right_out = right_out.at[slot_ids, row_slice].set(right_new)
        left_basis_out = left_basis_out.at[slot_ids, row_slice].set(left_fresh)
        right_basis_out = right_basis_out.at[slot_ids, row_slice].set(right_fresh)
    update = jnp.concatenate(pieces, axis=2)
    return (update, left_out, right_out, left_basis_out, right_basis_out)
```

```python
import functools
import math

import jax
import jax.numpy as jnp
from jax import lax
from jax.experimental import pallas as pl
from jax.experimental.pallas import tpu as pltpu
from jax.sharding import PartitionSpec as P

NSTEPS = 6
BETA = 0.9
EPS = 1e-06
HIGHEST = lax.Precision.HIGHEST
MESH = pl.DeviceIdType.MESH
NX, NY, NZ, NQ = 4, 4, 8, 32
BLK = 256
RA, RB = 160, 128
SPARE = 8
PIECES = 6
PROWS = 128


def place():
    dp = lax.axis_index("dp")
    x = lax.axis_index("mp")
    return x, lax.rem(lax.div(dp, 2), NY), lax.div(dp, 2 * NY), lax.rem(dp, 2)


def device(dx=0, dy=0, dz=0, dc=0):
    x, y, z, c = place()
    x = lax.rem(x + dx + NX, NX)
    y = lax.rem(y + dy + NY, NY)
    z = lax.rem(z + dz + NZ, NZ)
    c = lax.rem(c + dc, 2)
    return ((z * NY + y) * 2 + c, x)


def remote(src, dst, send, recv, target):
    return pltpu.make_async_remote_copy(
        src_ref=src, dst_ref=dst, send_sem=send, recv_sem=recv, device_id=target, device_id_type=MESH
    )


def encode(read, groups, dst):
    exponents = []
    for g in range(groups):
        value = read(g)
        top = jnp.max(jnp.abs(value), axis=0, keepdims=True)
        exponent = jnp.ceil(jnp.log2(jnp.maximum(top, 1e-30) * (1.0 / 32700.0)))
        exponents.append(exponent)
        coded = jnp.round(value * jnp.exp2(-exponent))
        dst[pl.ds(16 * g, 16), :] = coded.astype(jnp.int32).astype(jnp.int16)
    exponents.append(jnp.zeros((16 - groups, BLK), jnp.float32))
    tile = jnp.concatenate(exponents, axis=0)
    dst[pl.ds(16 * groups, 16), :] = tile.astype(jnp.int32).astype(jnp.int16)


def decoder(src, groups):
    scales = jnp.exp2(src[pl.ds(16 * groups, 16), :].astype(jnp.int32).astype(jnp.float32))

    def read(g):
        value = src[pl.ds(16 * g, 16), :].astype(jnp.int32).astype(jnp.float32)
        return value * scales[g : g + 1, :]

    return read


def gradient_kernel(
    token_scale,
    owner_ref,
    act_ref,
    cot_ref,
    primary_ref,
    second_ref,
    table_v,
    table_s,
    at,
    cot2,
    part,
    spill,
    ya2_s,
    ya2_r,
    ya1_s,
    ya1_r,
    za4_s,
    za4_r,
    za_s,
    za_r,
    zb4_s,
    zb4_r,
    zb_s,
    zb_r,
    yb2_s,
    yb2_r,
    yb1_s,
    yb1_r,
    sec,
    sec_out,
    sec_in,
    x_send,
    x_recv,
    f_send,
    f_recv,
    c_send,
    c_recv,
    ya2_sem,
    ya1_sem,
    za4_sem,
    za_sem,
    zb4_sem,
    zb_sem,
    yb2_sem,
    yb1_sem,
    t_sem,
    s_sem,
):
    x, y, z, c = place()
    me_q = z * NY + y
    other = device(dc=1)

    barrier = pltpu.get_barrier_semaphore()
    for target in (device(dx=1), device(dx=3), other):
        pl.semaphore_signal(barrier, inc=1, device_id=target, device_id_type=MESH)

    @pl.loop(1, NQ)
    def _(r):
        q = lax.rem(me_q + r, NQ)
        pl.semaphore_signal(barrier, inc=1, device_id=(q * 2 + c, x), device_id_type=MESH)

    def piece(half, shard, p):
        return at.at[half, 3 * shard + p // 2, pl.ds((p % 2) * PROWS, PROWS), :]

    def turn(p):
        at[0, p // 2, pl.ds((p % 2) * PROWS, PROWS), :] = act_ref[:, pl.ds(p * PROWS, PROWS)].T

    order = (0, 5, 1, 4, 2, 3)
    turn(order[0])
    pl.semaphore_wait(barrier, NQ + 2)

    def own_piece(p, d):
        sgn = 1 - 2 * d
        return remote(
            piece(0, 0, p), piece(0, (4 - sgn) % 4, p), x_send.at[d, p], x_recv.at[d, p], device(dx=sgn)
        )

    def forward_piece(p, d):
        sgn = 1 - 2 * d
        return remote(piece(0, (4 - sgn) % 4, p), piece(0, 2, p), f_send.at[p], f_recv.at[p], device(dx=sgn))

    def core_shard(r, sem):
        rows = pl.ds(3 * r, 3)
        return remote(at.at[0, rows], at.at[1, rows], c_send.at[sem], c_recv.at[sem], other)

    def core_piece(p):
        return remote(piece(0, 2, p), piece(1, 2, p), c_send.at[4 + p], c_recv.at[4 + p], other)

    for n, p in enumerate(order):
        if n > 0:
            turn(p)
        own_piece(p, 0).start()
        own_piece(p, 1).start()
    core_shard(0, 1).start()
    for j in range(6):
        cot2[0, j] = cot_ref[:, pl.ds(j * BLK, BLK)]
    cot_copy = remote(cot2.at[0], cot2.at[1], c_send.at[0], c_recv.at[0], other)
    cot_copy.start()

    owners = owner_ref[...]
    lanes = lax.broadcasted_iota(jnp.int32, (128, 128), 1)
    subs = lax.broadcasted_iota(jnp.int32, (128, 128), 0)
    earlier = lanes < subs
    same = jnp.broadcast_to(owners, (128, 128)).T == owners
    is_second = jnp.max(jnp.where(same & earlier & (subs < 72), 1, 0), axis=1, keepdims=True)
    is_second = jnp.broadcast_to(is_second, (128, 128))
    second_row = is_second.T
    rank = jnp.sum(jnp.where(earlier, second_row, 0), axis=1, keepdims=True)
    rank = jnp.broadcast_to(rank, (128, 128))
    rank_row = rank.T
    mine = owners == subs
    first = jnp.min(jnp.where(mine, lanes, 71), axis=1, keepdims=True)
    entry = jnp.sum(jnp.where(mine, second_row * rank_row, 0), axis=1, keepdims=True)
    numbers = jnp.sum(jnp.where(rank == lanes, is_second * subs, 0), axis=0, keepdims=True)
    entry = jnp.minimum(entry, SPARE - 1)
    table_v[...] = jnp.where(subs == 64, numbers, jnp.where(lanes == 0, first, entry))
    table_copy = pltpu.make_async_copy(table_v, table_s, t_sem)
    table_copy.start()
    table_copy.wait()

    for n in range(3):
        own_piece(n, 0).wait_recv()
        forward_piece(n, 0).start()
        own_piece(5 - n, 1).wait_recv()
        forward_piece(5 - n, 1).start()
    for n in range(3, 6):
        own_piece(n, 0).wait_recv()
        own_piece(5 - n, 1).wait_recv()
    core_shard(3, 2).start()
    core_shard(1, 3).start()
    for n in range(3):
        forward_piece(n, 0).wait_recv()
        core_piece(n).start()
        forward_piece(5 - n, 1).wait_recv()
        core_piece(5 - n).start()
    cot_copy.wait_recv()
    core_shard(0, 1).wait_recv()
    core_shard(3, 2).wait_recv()
    core_shard(1, 3).wait_recv()
    for p in range(PIECES):
        core_piece(p).wait_recv()

    def product_of(block):
        band = lax.rem(lax.div(block, 6) - 3 * x + 12, 12)
        column = lax.rem(block, 6)
        total = jnp.dot(at[0, band], cot2[0, column], preferred_element_type=jnp.float32)
        total += jnp.dot(at[1, band], cot2[1, column], preferred_element_type=jnp.float32)
        return total * token_scale

    @pl.loop(0, SPARE // 2)
    def _(s):
        spill[...] = product_of(table_s[64, 2 * s + c]).reshape(NQ, 8, BLK)

        @pl.loop(0, NQ)
        def _(q):
            dz = lax.rem(lax.div(q, NY) - z + NZ, NZ)
            dy = lax.rem(lax.rem(q, NY) - y + NY, NY)
            part[dz, dy, pl.ds(pl.multiple_of(BLK + 8 * s, 8), 8), :] = spill[q]

    def produce(dz):
        @pl.loop(0, NY)
        def _(dy):
            q = lax.rem(z + dz, NZ) * NY + lax.rem(y + dy, NY)
            part[dz, dy, pl.ds(0, BLK), :] = product_of(table_s[2 * q + c, 0])

    def rows_of(dz, dy, start):
        def read(g):
            return part[dz, dy, pl.ds(start + 16 * g, 16), :]

        return read

    def both(first_read, second_read, low=0, high=1000):
        def read(g):
            if low <= g < high:
                return first_read(g) + second_read(g - low)
            return first_read(g)

        return read

    def hop(src, dst, sems, index, target):
        return remote(src.at[index], dst.at[index], sems.at[(0,) + index], sems.at[(1,) + index], target)

    def y_target(d):
        return device(dy=1 - 2 * d)

    def z_target(d):
        return device(dz=1 - 2 * d)

    GA, GB = RA // 16, RB // 16

    def dirs(body):
        for d in range(2):
            body(d)

    def a_y2(dz):
        def body(d):
            encode(rows_of(dz, 2, d * (RA // 2)), GA // 2, ya2_s.at[dz, d])
            hop(ya2_s, ya2_r, ya2_sem, (dz, d), y_target(d)).start()

        dirs(body)

    def a_y1(dz):
        def body(d):
            hop(ya2_s, ya2_r, ya2_sem, (dz, d), y_target(d)).wait_recv()
            arrived = decoder(ya2_r.at[dz, d], GA // 2)
            low = d * (GA // 2)
            encode(both(rows_of(dz, 1 + 2 * d, 0), arrived, low, low + GA // 2), GA, ya1_s.at[dz, d])
            hop(ya1_s, ya1_r, ya1_sem, (dz, d), y_target(d)).start()

        dirs(body)

    def a_yf(dz):
        for d in range(2):
            hop(ya1_s, ya1_r, ya1_sem, (dz, d), y_target(d)).wait_recv()
        left, right = decoder(ya1_r.at[dz, 0], GA), decoder(ya1_r.at[dz, 1], GA)
        for g in range(GA):
            part[dz, 0, pl.ds(16 * g, 16), :] += left(g) + right(g)

    def a_z(k):
        def body(d):
            if k == 4:
                encode(rows_of(4, 0, d * (RA // 2)), GA // 2, za4_s.at[d])
                hop(za4_s, za4_r, za4_sem, (d,), z_target(d)).start()
                return
            dz = k if d == 0 else 8 - k
            if k == 3:
                hop(za4_s, za4_r, za4_sem, (d,), z_target(d)).wait_recv()
                low = d * (GA // 2)
                read = both(rows_of(dz, 0, 0), decoder(za4_r.at[d], GA // 2), low, low + GA // 2)
            else:
                hop(za_s, za_r, za_sem, (k, d), z_target(d)).wait_recv()
                read = both(rows_of(dz, 0, 0), decoder(za_r.at[k, d], GA))
            encode(read, GA, za_s.at[k - 1, d])
            hop(za_s, za_r, za_sem, (k - 1, d), z_target(d)).start()

        dirs(body)

    def b_z(k):
        @pl.loop(0, NY)
        def _(n):
            dy = lax.rem(n + 2, NY)

            def body(d):
                if k == 4:
                    encode(rows_of(4, dy, RA + d * (RB // 2)), GB // 2, zb4_s.at[dy, d])
                    hop(zb4_s, zb4_r, zb4_sem, (dy, d), z_target(d)).start()
                    return
                dz = k if d == 0 else 8 - k
                if k == 3:
                    hop(zb4_s, zb4_r, zb4_sem, (dy, d), z_target(d)).wait_recv()
                    low = d * (GB // 2)
                    read = both(rows_of(dz, dy, RA), decoder(zb4_r.at[dy, d], GB // 2), low, low + GB // 2)
                else:
                    hop(zb_s, zb_r, zb_sem, (k, dy, d), z_target(d)).wait_recv()
                    read = both(rows_of(dz, dy, RA), decoder(zb_r.at[k, dy, d], GB))
                encode(read, GB, zb_s.at[k - 1, dy, d])
                hop(zb_s, zb_r, zb_sem, (k - 1, dy, d), z_target(d)).start()

            dirs(body)

    def b_zf(dy):
        for d in range(2):
            hop(zb_s, zb_r, zb_sem, (0, dy, d), z_target(d)).wait_recv()
        left, right = decoder(zb_r.at[0, dy, 0], GB), decoder(zb_r.at[0, dy, 1], GB)
        for g in range(GB):
            part[0, dy, pl.ds(RA + 16 * g, 16), :] += left(g) + right(g)

    def b_y2():
        def body(d):
            encode(rows_of(0, 2, RA + d * (RB // 2)), GB // 2, yb2_s.at[d])
            hop(yb2_s, yb2_r, yb2_sem, (d,), y_target(d)).start()

        dirs(body)

    def b_y1():
        def body(d):
            hop(yb2_s, yb2_r, yb2_sem, (d,), y_target(d)).wait_recv()
            arrived = decoder(yb2_r.at[d], GB // 2)
            low = d * (GB // 2)
            encode(both(rows_of(0, 1 + 2 * d, RA), arrived, low, low + GB // 2), GB, yb1_s.at[d])
            hop(yb1_s, yb1_r, yb1_sem, (d,), y_target(d)).start()

        dirs(body)

    produce(4)
    b_z(4)
    a_y2(4)
    produce(3)
    produce(5)
    a_y2(3)
    a_y2(5)
    b_z(3)
    a_y1(4)
    produce(2)
    produce(6)
    a_y2(2)
    a_y2(6)
    a_y1(3)
    a_y1(5)
    b_z(2)
    a_yf(4)
    a_z(4)
    produce(1)
    produce(7)
    a_y2(1)
    a_y2(7)
    a_y1(2)
    a_y1(6)
    a_yf(3)
    a_yf(5)
    a_z(3)
    b_z(1)
    produce(0)
    a_y2(0)
    a_y1(1)
    a_y1(7)
    a_yf(2)
    a_yf(6)
    a_z(2)
    b_zf(2)
    b_y2()
    a_y1(0)
    a_yf(1)
    a_yf(7)
    a_z(1)
    b_zf(1)
    b_zf(3)
    b_y1()
    b_zf(0)
    a_yf(0)

    for d in range(2):
        hop(yb1_s, yb1_r, yb1_sem, (d,), y_target(d)).wait_recv()
    left, right = decoder(yb1_r.at[0], GB), decoder(yb1_r.at[1], GB)
    for g in range(GB):
        rows = part[0, 0, pl.ds(RA + 16 * g, 16), :] + left(g) + right(g)
        if g < 6:
            primary_ref[pl.ds(RA + 16 * g, 16), :] = rows
        else:
            sec[c, pl.ds(2 * (g - 6), 2)] = rows.reshape(2, 8, BLK)
    sec_copy = remote(sec.at[c], sec.at[c], s_sem.at[0], s_sem.at[1], other)
    sec_copy.start()

    for d in range(2):
        hop(za_s, za_r, za_sem, (0, d), z_target(d)).wait_recv()
    left, right = decoder(za_r.at[0, 0], GA), decoder(za_r.at[0, 1], GA)
    for g in range(GA):
        primary_ref[pl.ds(16 * g, 16), :] = part[0, 0, pl.ds(16 * g, 16), :] + left(g) + right(g)

    sec_copy.wait_recv()

    @pl.loop(0, NQ)
    def _(q):
        place_of = table_s[2 * q + c, 1]
        sec_out[q] = sec[lax.rem(place_of, 2), lax.div(place_of, 2)]

    @pl.loop(1, NQ)
    def _(r):
        q = lax.rem(me_q + r, NQ)
        remote(sec_out.at[q], sec_in.at[me_q], s_sem.at[2], s_sem.at[3], (q * 2 + c, x)).start()

    whole = remote(sec_out.at[pl.ds(0, NQ - 1)], sec_in.at[pl.ds(0, NQ - 1)], s_sem.at[2], s_sem.at[3], other)
    whole.wait_recv()
    second_ref[...] = sec_in[...]
    second_ref[me_q] = sec_out[me_q]

    whole.wait_send()
    sec_copy.wait_send()
    cot_copy.wait_send()
    core_shard(0, 1).wait_send()
    core_shard(3, 2).wait_send()
    core_shard(1, 3).wait_send()
    for p in range(PIECES):
        core_piece(p).wait_send()
        own_piece(p, 0).wait_send()
        own_piece(p, 1).wait_send()
        forward_piece(p, 0 if p < 3 else 1).wait_send()
    for d in range(2):
        for dz in range(NZ):
            hop(ya2_s, ya2_r, ya2_sem, (dz, d), y_target(d)).wait_send()
            hop(ya1_s, ya1_r, ya1_sem, (dz, d), y_target(d)).wait_send()
        hop(za4_s, za4_r, za4_sem, (d,), z_target(d)).wait_send()
        hop(yb2_s, yb2_r, yb2_sem, (d,), y_target(d)).wait_send()
        hop(yb1_s, yb1_r, yb1_sem, (d,), y_target(d)).wait_send()
        for k in range(3):
            hop(za_s, za_r, za_sem, (k, d), z_target(d)).wait_send()
            for dy in range(NY):
                hop(zb_s, zb_r, zb_sem, (k, dy, d), z_target(d)).wait_send()
        for dy in range(NY):
            hop(zb4_s, zb4_r, zb4_sem, (dy, d), z_target(d)).wait_send()


def owner_gradients(activations, cotangent, block_owner, token_scale):
    owner_row = jnp.pad(block_owner, (0, 56), constant_values=-1).reshape(1, 128)
    i16, f32, i32, bf16 = jnp.int16, jnp.float32, jnp.int32, jnp.bfloat16
    vmem, dma = pltpu.VMEM, pltpu.SemaphoreType.DMA

    def pair(shape):
        return [vmem(shape, i16), vmem(shape, i16)]

    ha, hb = RA // 2 + 16, RB // 2 + 16
    fa, fb = RA + 16, RB + 16
    return pl.pallas_call(
        functools.partial(gradient_kernel, token_scale),
        out_shape=(
            jax.ShapeDtypeStruct((BLK, BLK), f32),
            jax.ShapeDtypeStruct((NQ, 8, BLK), f32),
        ),
        in_specs=[pl.BlockSpec(memory_space=pltpu.VMEM)] * 3,
        out_specs=[pl.BlockSpec(memory_space=pltpu.VMEM)] * 2,
        scratch_shapes=[
            vmem((128, 128), i32),
            pltpu.SMEM((128, 128), i32),
            vmem((2, 3 * NX, BLK, 512), bf16),
            vmem((2, 6, 512, BLK), bf16),
            vmem((NZ, NY, RA + RB, BLK), f32),
            vmem((NQ, 8, BLK), f32),
        ]
        + pair((NZ, 2, ha, BLK))
        + pair((NZ, 2, fa, BLK))
        + pair((2, ha, BLK))
        + pair((3, 2, fa, BLK))
        + pair((NY, 2, hb, BLK))
        + pair((3, NY, 2, fb, BLK))
        + pair((2, hb, BLK))
        + pair((2, fb, BLK))
        + [
            vmem((2, SPARE // 2, 8, BLK), f32),
            vmem((NQ, 8, BLK), f32),
            vmem((NQ, 8, BLK), f32),
            dma((2, PIECES)),
            dma((2, PIECES)),
            dma((PIECES,)),
            dma((PIECES,)),
            dma((10,)),
            dma((10,)),
            dma((2, NZ, 2)),
            dma((2, NZ, 2)),
            dma((2, 2)),
            dma((2, 3, 2)),
            dma((2, NY, 2)),
            dma((2, 3, NY, 2)),
            dma((2, 2)),
            dma((2, 2)),
            dma,
            dma((4,)),
        ],
        compiler_params=pltpu.CompilerParams(
            collective_id=0, has_side_effects=True, vmem_limit_bytes=48 * 1024 * 1024
        ),
    )(owner_row, activations, cotangent)


def product(left_side, right_side):
    return jnp.dot(left_side, right_side, precision=HIGHEST, preferred_element_type=jnp.float32)


def orthogonalize(matrix):
    current = matrix / jnp.sqrt(jnp.sum(matrix * matrix) + EPS)
    identity = jnp.eye(matrix.shape[0], dtype=jnp.float32)
    for _ in range(NSTEPS):
        current = product(current, 1.5 * identity - 0.5 * product(current.T, current))
    return current


def refresh(gradient, left_old, right_old, left_prev, right_prev):
    order_size = gradient.shape[0]
    left_new = BETA * left_old + (1.0 - BETA) / order_size * product(gradient, gradient.T)
    right_new = BETA * right_old + (1.0 - BETA) / order_size * product(gradient.T, gradient)
    left_power = product(left_new, left_prev)
    right_power = product(right_new, right_prev)
    left_fresh = orthogonalize(left_power)
    right_fresh = orthogonalize(right_power)
    left_scale = (jnp.mean(left_power * left_power, axis=0) + EPS) ** (-0.125)
    right_scale = (jnp.mean(right_power * right_power, axis=0) + EPS) ** (-0.125)
    rotated = product(product(left_fresh.T, gradient), right_fresh)
    rotated = rotated * left_scale[:, None] * right_scale[None, :]
    block_update = product(product(left_fresh, rotated), right_fresh.T).astype(jnp.bfloat16)
    return (block_update, left_new, right_new, left_fresh, right_fresh)


def slot_numbers(block_owner, capacity):
    positions = jnp.arange(block_owner.shape[0], dtype=jnp.int32)
    same_owner = block_owner[:, None] == block_owner[None, :]
    earlier = positions[None, :] < positions[:, None]
    slot_rank = jnp.sum(jnp.where(same_owner & earlier, 1, 0), axis=1).astype(jnp.int32)
    return block_owner * capacity + slot_rank


def on_device(
    activations, cotangent, block_owner, left_factor, right_factor, left_basis, right_basis
):
    dp_count = lax.axis_size("dp")
    token_scale = 1.0 / math.sqrt(activations.shape[0] * dp_count)
    slot_ids = slot_numbers(block_owner, 2)
    primary, second = owner_gradients(activations, cotangent, block_owner, token_scale)
    own_index = lax.axis_index("dp")
    held = jnp.sum(jnp.where(block_owner == own_index, 1, 0))
    live_here = jnp.stack([held > 0, held > 1])
    owned_blocks = jnp.stack([primary, second.reshape(BLK, BLK)])

    def handle_slot(unused_carry, slot_entry):
        is_live = slot_entry[0]
        operands = slot_entry[1:]

        def refresh_slot(values):
            return refresh(*values)

        def skip_slot(values):
            return (
                jnp.zeros(values[0].shape, jnp.bfloat16),
                values[1],
                values[2],
                values[3],
                values[4],
            )

        return (unused_carry, lax.cond(is_live, refresh_slot, skip_slot, operands))

    _, results = lax.scan(
        handle_slot,
        jnp.zeros((), jnp.int32),
        (live_here, owned_blocks, left_factor, right_factor, left_basis, right_basis),
    )
    updates, left_next, right_next, left_basis_next, right_basis_next = results
    outgoing = jnp.swapaxes(updates, 0, 1)
    returned = lax.all_to_all(outgoing, "dp", split_axis=0, concat_axis=1, tiled=True)
    own_rows = jnp.take(returned, slot_ids, axis=1)
    update = own_rows.reshape(own_rows.shape[0], 12, 1536)
    return (update, left_next, right_next, left_basis_next, right_basis_next)


def solution(mesh):
    placed = (
        P("dp", "mp"),
        P("dp", "mp"),
        P(),
        P("dp", "mp", None),
        P("dp", "mp", None),
        P("dp", "mp", None),
        P("dp", "mp", None),
    )
    return jax.shard_map(
        on_device,
        mesh=mesh,
        in_specs=placed,
        out_specs=(
            P("dp", None, "mp"),
            P("dp", "mp", None),
            P("dp", "mp", None),
            P("dp", "mp", None),
            P("dp", "mp", None),
        ),
        check_vma=False,
    )
```

```python
import functools
import math

import jax
import jax.numpy as jnp
from jax import lax
from jax.experimental import pallas as pl
from jax.experimental.pallas import tpu as pltpu
from jax.sharding import PartitionSpec as P

NSTEPS = 6
BETA = 0.9
EPS = 1e-06
MESH = pl.DeviceIdType.MESH
NX, NY, NZ, NQ = 4, 4, 8, 32
BLK = 256
RA, RB = 160, 128
SPARE = 8
PIECES = 6
PROWS = 128


def place():
    dp = lax.axis_index("dp")
    x = lax.axis_index("mp")
    return x, lax.rem(lax.div(dp, 2), NY), lax.div(dp, 2 * NY), lax.rem(dp, 2)


def device(dx=0, dy=0, dz=0, dc=0):
    x, y, z, c = place()
    x = lax.rem(x + dx + NX, NX)
    y = lax.rem(y + dy + NY, NY)
    z = lax.rem(z + dz + NZ, NZ)
    c = lax.rem(c + dc, 2)
    return ((z * NY + y) * 2 + c, x)


def remote(src, dst, send, recv, target):
    return pltpu.make_async_remote_copy(
        src_ref=src, dst_ref=dst, send_sem=send, recv_sem=recv, device_id=target, device_id_type=MESH
    )


def encode(read, groups, dst):
    exponents = []
    for g in range(groups):
        value = read(g)
        top = jnp.max(jnp.abs(value), axis=0, keepdims=True)
        exponent = jnp.ceil(jnp.log2(jnp.maximum(top, 1e-30) * (1.0 / 32700.0)))
        exponents.append(exponent)
        coded = jnp.round(value * jnp.exp2(-exponent))
        dst[pl.ds(16 * g, 16), :] = coded.astype(jnp.int32).astype(jnp.int16)
    exponents.append(jnp.zeros((16 - groups, BLK), jnp.float32))
    tile = jnp.concatenate(exponents, axis=0)
    dst[pl.ds(16 * groups, 16), :] = tile.astype(jnp.int32).astype(jnp.int16)


def decoder(src, groups):
    scales = jnp.exp2(src[pl.ds(16 * groups, 16), :].astype(jnp.int32).astype(jnp.float32))

    def read(g):
        value = src[pl.ds(16 * g, 16), :].astype(jnp.int32).astype(jnp.float32)
        return value * scales[g : g + 1, :]

    return read


def split(value):
    high = value.astype(jnp.bfloat16)
    return high, (value - high.astype(jnp.float32)).astype(jnp.bfloat16)


def turned(parts):
    return parts[0].T, parts[1].T


def times(left_parts, right_parts):
    def dot(a, b):
        return jnp.dot(a, b, preferred_element_type=jnp.float32)

    low = dot(left_parts[1], right_parts[0]) + dot(left_parts[0], right_parts[1])
    return dot(left_parts[0], right_parts[0]) + low


def refresh(gradient, held, fresh, k, live):
    def keep(n, value):
        fresh[n, k] = value if live is None else jnp.where(live, value, held[n, k])

    g = split(gradient)
    gt = turned(g)
    share = (1.0 - BETA) / BLK
    factors = [BETA * held[0, k] + share * times(g, gt), BETA * held[1, k] + share * times(gt, g)]
    powers, scales = [], []
    for n in range(2):
        keep(n, factors[n])
        power = times(split(factors[n]), split(held[2 + n, k]))
        square = jnp.sum(power * power, axis=0, keepdims=True)
        scales.append(jnp.exp(-0.125 * jnp.log(square * (1.0 / BLK) + EPS)))
        powers.append(power / jnp.sqrt(jnp.sum(square, axis=1, keepdims=True) + EPS))

    def step(_, values):
        parts = [split(v) for v in values]
        grams = [times(turned(p), p) for p in parts]
        moves = [times(p, split(gram)) for p, gram in zip(parts, grams)]
        return tuple(1.5 * v - 0.5 * m for v, m in zip(values, moves))

    bases = lax.fori_loop(0, NSTEPS, step, tuple(powers))
    weights = []
    for n in range(2):
        keep(2 + n, bases[n])
        weights.append(times(split(bases[n] * scales[n]), turned(split(bases[n]))))
    inner = times(g, split(weights[1]))
    return times(split(weights[0]), split(inner))


def gradient_kernel(
    token_scale,
    owner_ref,
    act_hbm,
    cot_hbm,
    left_hbm,
    right_hbm,
    left_basis_hbm,
    right_basis_hbm,
    update_ref,
    left_out,
    right_out,
    left_basis_out,
    right_basis_out,
    owner_v,
    act_ref,
    held,
    fresh,
    grad,
    u_send,
    ret,
    stage,
    table_v,
    table_s,
    at,
    cot2,
    part,
    spill,
    ya2_s,
    ya2_r,
    ya1_s,
    ya1_r,
    za4_s,
    za4_r,
    za_s,
    za_r,
    zb4_s,
    zb4_r,
    zb_s,
    zb_r,
    yb2_s,
    yb2_r,
    yb1_s,
    yb1_r,
    sec,
    sec_out,
    sec_in,
    x_send,
    x_recv,
    f_send,
    f_recv,
    c_send,
    c_recv,
    ya2_sem,
    ya1_sem,
    za4_sem,
    za_sem,
    zb4_sem,
    zb_sem,
    yb2_sem,
    yb1_sem,
    t_sem,
    s_sem,
    in_sem,
    held_sem,
    out_sem,
    u_sem,
    r_sem,
):
    x, y, z, c = place()
    me_q = z * NY + y
    other = device(dc=1)

    def act_in(n):
        columns = pl.ds(n * 384, 384)
        return pltpu.make_async_copy(act_hbm.at[:, columns], act_ref.at[:, columns], in_sem.at[6 + n])

    def cot_in(j):
        return pltpu.make_async_copy(cot_hbm.at[:, pl.ds(j * BLK, BLK)], cot2.at[0, j], in_sem.at[j])

    factors = (left_hbm, right_hbm, left_basis_hbm, right_basis_hbm)
    results = (left_out, right_out, left_basis_out, right_basis_out)

    def held_in(n):
        return pltpu.make_async_copy(factors[n], held.at[n], held_sem.at[n])

    def fresh_out(n, k):
        return pltpu.make_async_copy(fresh.at[n, k], results[n].at[k], out_sem.at[n, k])

    act_in(0).start()
    act_in(1).start()
    for j in range(6):
        cot_in(j).start()
    for n in range(4):
        held_in(n).start()

    barrier = pltpu.get_barrier_semaphore()
    for target in (device(dx=1), device(dx=3), other):
        pl.semaphore_signal(barrier, inc=1, device_id=target, device_id_type=MESH)

    @pl.loop(1, NQ)
    def _(r):
        q = lax.rem(me_q + r, NQ)
        pl.semaphore_signal(barrier, inc=1, device_id=(q * 2 + c, x), device_id_type=MESH)

    def piece(half, shard, p):
        return at.at[half, 3 * shard + p // 2, pl.ds((p % 2) * PROWS, PROWS), :]

    def turn(p):
        at[0, p // 2, pl.ds((p % 2) * PROWS, PROWS), :] = act_ref[:, pl.ds(p * PROWS, PROWS)].T

    order = (0, 5, 1, 4, 2, 3)
    act_in(0).wait()
    act_in(1).wait()
    turn(order[0])
    pl.semaphore_wait(barrier, NQ + 2)

    def own_piece(p, d):
        sgn = 1 - 2 * d
        return remote(
            piece(0, 0, p), piece(0, (4 - sgn) % 4, p), x_send.at[d, p], x_recv.at[d, p], device(dx=sgn)
        )

    def forward_piece(p, d):
        sgn = 1 - 2 * d
        return remote(piece(0, (4 - sgn) % 4, p), piece(0, 2, p), f_send.at[p], f_recv.at[p], device(dx=sgn))

    def core_shard(r, sem):
        rows = pl.ds(3 * r, 3)
        return remote(at.at[0, rows], at.at[1, rows], c_send.at[sem], c_recv.at[sem], other)

    def core_piece(p):
        return remote(piece(0, 2, p), piece(1, 2, p), c_send.at[4 + p], c_recv.at[4 + p], other)

    for n, p in enumerate(order):
        if n > 0:
            turn(p)
        own_piece(p, 0).start()
        own_piece(p, 1).start()
    core_shard(0, 1).start()
    for j in range(6):
        cot_in(j).wait()
    cot_copy = remote(cot2.at[0], cot2.at[1], c_send.at[0], c_recv.at[0], other)
    cot_copy.start()

    owner_v[...] = jnp.full((1, 128), -1, jnp.int32)
    owner_v[:, pl.ds(0, 72)] = owner_ref[...]
    owners = owner_v[...]
    lanes = lax.broadcasted_iota(jnp.int32, (128, 128), 1)
    subs = lax.broadcasted_iota(jnp.int32, (128, 128), 0)
    earlier = lanes < subs
    owner_column = jnp.broadcast_to(owners, (128, 128)).T
    same = owner_column == owners
    is_second = jnp.max(jnp.where(same & earlier & (subs < 72), 1, 0), axis=1, keepdims=True)
    is_second = jnp.broadcast_to(is_second, (128, 128))
    second_row = is_second.T
    rank = jnp.sum(jnp.where(earlier, second_row, 0), axis=1, keepdims=True)
    rank = jnp.broadcast_to(rank, (128, 128))
    rank_row = rank.T
    mine = owners == subs
    first = jnp.min(jnp.where(mine, lanes, 71), axis=1, keepdims=True)
    entry = jnp.sum(jnp.where(mine, second_row * rank_row, 0), axis=1, keepdims=True)
    numbers = jnp.sum(jnp.where(rank == lanes, is_second * subs, 0), axis=0, keepdims=True)
    entry = jnp.minimum(entry, SPARE - 1)
    count = jnp.sum(jnp.where(mine, 1, 0), axis=1, keepdims=True)
    slots = jnp.where(subs < 72, 2 * owner_column + is_second, 0)
    columns = jnp.where(lanes == 0, first, jnp.where(lanes == 1, entry, jnp.where(lanes == 2, slots, count)))
    table_v[0:128, :] = columns
    table_v[128:136, :] = jnp.broadcast_to(numbers, (8, 128))
    table_copy = pltpu.make_async_copy(table_v, table_s, t_sem)
    table_copy.start()
    table_copy.wait()

    for n in range(3):
        own_piece(n, 0).wait_recv()
        forward_piece(n, 0).start()
        own_piece(5 - n, 1).wait_recv()
        forward_piece(5 - n, 1).start()
    for n in range(3, 6):
        own_piece(n, 0).wait_recv()
        own_piece(5 - n, 1).wait_recv()
    core_shard(3, 2).start()
    core_shard(1, 3).start()
    for n in range(3):
        forward_piece(n, 0).wait_recv()
        core_piece(n).start()
        forward_piece(5 - n, 1).wait_recv()
        core_piece(5 - n).start()
    cot_copy.wait_recv()
    core_shard(0, 1).wait_recv()
    core_shard(3, 2).wait_recv()
    core_shard(1, 3).wait_recv()
    for p in range(PIECES):
        core_piece(p).wait_recv()

    def product_of(block):
        band = lax.rem(lax.div(block, 6) - 3 * x + 12, 12)
        column = lax.rem(block, 6)
        total = jnp.dot(at[0, band], cot2[0, column], preferred_element_type=jnp.float32)
        total += jnp.dot(at[1, band], cot2[1, column], preferred_element_type=jnp.float32)
        return total * token_scale

    @pl.loop(0, SPARE // 2)
    def _(s):
        spill[...] = product_of(table_s[128, 2 * s + c]).reshape(NQ, 8, BLK)

        @pl.loop(0, NQ)
        def _(q):
            dz = lax.rem(lax.div(q, NY) - z + NZ, NZ)
            dy = lax.rem(lax.rem(q, NY) - y + NY, NY)
            part[dz, dy, pl.ds(pl.multiple_of(BLK + 8 * s, 8), 8), :] = spill[q]

    def produce(dz):
        @pl.loop(0, NY)
        def _(dy):
            q = lax.rem(z + dz, NZ) * NY + lax.rem(y + dy, NY)
            part[dz, dy, pl.ds(0, BLK), :] = product_of(table_s[2 * q + c, 0])

    def rows_of(dz, dy, start):
        def read(g):
            return part[dz, dy, pl.ds(start + 16 * g, 16), :]

        return read

    def both(first_read, second_read, low=0, high=1000):
        def read(g):
            if low <= g < high:
                return first_read(g) + second_read(g - low)
            return first_read(g)

        return read

    def hop(src, dst, sems, index, target):
        return remote(src.at[index], dst.at[index], sems.at[(0,) + index], sems.at[(1,) + index], target)

    def y_target(d):
        return device(dy=1 - 2 * d)

    def z_target(d):
        return device(dz=1 - 2 * d)

    GA, GB = RA // 16, RB // 16

    def dirs(body):
        for d in range(2):
            body(d)

    def a_y2(dz):
        def body(d):
            encode(rows_of(dz, 2, d * (RA // 2)), GA // 2, ya2_s.at[dz, d])
            hop(ya2_s, ya2_r, ya2_sem, (dz, d), y_target(d)).start()

        dirs(body)

    def a_y1(dz):
        def body(d):
            hop(ya2_s, ya2_r, ya2_sem, (dz, d), y_target(d)).wait_recv()
            arrived = decoder(ya2_r.at[dz, d], GA // 2)
            low = d * (GA // 2)
            encode(both(rows_of(dz, 1 + 2 * d, 0), arrived, low, low + GA // 2), GA, ya1_s.at[dz, d])
            hop(ya1_s, ya1_r, ya1_sem, (dz, d), y_target(d)).start()

        dirs(body)

    def a_yf(dz):
        for d in range(2):
            hop(ya1_s, ya1_r, ya1_sem, (dz, d), y_target(d)).wait_recv()
        left, right = decoder(ya1_r.at[dz, 0], GA), decoder(ya1_r.at[dz, 1], GA)
        for g in range(GA):
            part[dz, 0, pl.ds(16 * g, 16), :] += left(g) + right(g)

    def a_z(k):
        def body(d):
            if k == 4:
                encode(rows_of(4, 0, d * (RA // 2)), GA // 2, za4_s.at[d])
                hop(za4_s, za4_r, za4_sem, (d,), z_target(d)).start()
                return
            dz = k if d == 0 else 8 - k
            if k == 3:
                hop(za4_s, za4_r, za4_sem, (d,), z_target(d)).wait_recv()
                low = d * (GA // 2)
                read = both(rows_of(dz, 0, 0), decoder(za4_r.at[d], GA // 2), low, low + GA // 2)
            else:
                hop(za_s, za_r, za_sem, (k, d), z_target(d)).wait_recv()
                read = both(rows_of(dz, 0, 0), decoder(za_r.at[k, d], GA))
            encode(read, GA, za_s.at[k - 1, d])
            hop(za_s, za_r, za_sem, (k - 1, d), z_target(d)).start()

        dirs(body)

    def b_z(k):
        @pl.loop(0, NY)
        def _(n):
            dy = lax.rem(n + 2, NY)

            def body(d):
                if k == 4:
                    encode(rows_of(4, dy, RA + d * (RB // 2)), GB // 2, zb4_s.at[dy, d])
                    hop(zb4_s, zb4_r, zb4_sem, (dy, d), z_target(d)).start()
                    return
                dz = k if d == 0 else 8 - k
                if k == 3:
                    hop(zb4_s, zb4_r, zb4_sem, (dy, d), z_target(d)).wait_recv()
                    low = d * (GB // 2)
                    read = both(rows_of(dz, dy, RA), decoder(zb4_r.at[dy, d], GB // 2), low, low + GB // 2)
                else:
                    hop(zb_s, zb_r, zb_sem, (k, dy, d), z_target(d)).wait_recv()
                    read = both(rows_of(dz, dy, RA), decoder(zb_r.at[k, dy, d], GB))
                encode(read, GB, zb_s.at[k - 1, dy, d])
                hop(zb_s, zb_r, zb_sem, (k - 1, dy, d), z_target(d)).start()

            dirs(body)

    def b_zf(dy):
        for d in range(2):
            hop(zb_s, zb_r, zb_sem, (0, dy, d), z_target(d)).wait_recv()
        left, right = decoder(zb_r.at[0, dy, 0], GB), decoder(zb_r.at[0, dy, 1], GB)
        for g in range(GB):
            part[0, dy, pl.ds(RA + 16 * g, 16), :] += left(g) + right(g)

    def b_y2():
        def body(d):
            encode(rows_of(0, 2, RA + d * (RB // 2)), GB // 2, yb2_s.at[d])
            hop(yb2_s, yb2_r, yb2_sem, (d,), y_target(d)).start()

        dirs(body)

    def b_y1():
        def body(d):
            hop(yb2_s, yb2_r, yb2_sem, (d,), y_target(d)).wait_recv()
            arrived = decoder(yb2_r.at[d], GB // 2)
            low = d * (GB // 2)
            encode(both(rows_of(0, 1 + 2 * d, RA), arrived, low, low + GB // 2), GB, yb1_s.at[d])
            hop(yb1_s, yb1_r, yb1_sem, (d,), y_target(d)).start()

        dirs(body)

    produce(4)
    b_z(4)
    a_y2(4)
    produce(3)
    produce(5)
    a_y2(3)
    a_y2(5)
    b_z(3)
    a_y1(4)
    produce(2)
    produce(6)
    a_y2(2)
    a_y2(6)
    a_y1(3)
    a_y1(5)
    b_z(2)
    a_yf(4)
    a_z(4)
    produce(1)
    produce(7)
    a_y2(1)
    a_y2(7)
    a_y1(2)
    a_y1(6)
    a_yf(3)
    a_yf(5)
    a_z(3)
    b_z(1)
    produce(0)
    a_y2(0)
    a_y1(1)
    a_y1(7)
    a_yf(2)
    a_yf(6)
    a_z(2)
    b_zf(2)
    b_y2()
    a_y1(0)
    a_yf(1)
    a_yf(7)
    a_z(1)
    b_zf(1)
    b_zf(3)
    b_y1()
    b_zf(0)
    a_yf(0)

    for d in range(2):
        hop(yb1_s, yb1_r, yb1_sem, (d,), y_target(d)).wait_recv()
    left, right = decoder(yb1_r.at[0], GB), decoder(yb1_r.at[1], GB)
    for g in range(GB):
        rows = part[0, 0, pl.ds(RA + 16 * g, 16), :] + left(g) + right(g)
        if g < 6:
            grad[0, pl.ds(RA + 16 * g, 16), :] = rows
        else:
            sec[c, pl.ds(2 * (g - 6), 2)] = rows.reshape(2, 8, BLK)
    sec_copy = remote(sec.at[c], sec.at[c], s_sem.at[0], s_sem.at[1], other)
    sec_copy.start()

    for d in range(2):
        hop(za_s, za_r, za_sem, (0, d), z_target(d)).wait_recv()
    left, right = decoder(za_r.at[0, 0], GA), decoder(za_r.at[0, 1], GA)
    for g in range(GA):
        grad[0, pl.ds(16 * g, 16), :] = part[0, 0, pl.ds(16 * g, 16), :] + left(g) + right(g)

    sec_copy.wait_recv()

    @pl.loop(0, NQ)
    def _(q):
        place_of = table_s[2 * q + c, 1]
        sec_out[q] = sec[lax.rem(place_of, 2), lax.div(place_of, 2)]

    @pl.loop(1, NQ)
    def _(r):
        q = lax.rem(me_q + r, NQ)
        remote(sec_out.at[q], sec_in.at[me_q], s_sem.at[2], s_sem.at[3], (q * 2 + c, x)).start()

    whole = remote(sec_out.at[pl.ds(0, NQ - 1)], sec_in.at[pl.ds(0, NQ - 1)], s_sem.at[2], s_sem.at[3], other)
    for n in range(4):
        held_in(n).wait()

    def u_whole(k):
        part_of = pl.ds(0, NQ - 1)
        return remote(u_send.at[k, part_of], ret.at[k, c, part_of], u_sem.at[0, k], u_sem.at[1, k], other)

    def u_core(k):
        return remote(ret.at[k, c], ret.at[k, c], r_sem.at[0, k], r_sem.at[1, k], other)

    def finish(k):
        update = refresh(grad[k], held, fresh, k, None if k == 0 else table_s[me_q * 2 + c, 3] > 1)
        for n in range(4):
            fresh_out(n, k).start()
        rows = update.reshape(NQ, 8, BLK)
        halves = jnp.concatenate([rows[:, :, : BLK // 2], rows[:, :, BLK // 2 :]], axis=1)
        u_send[k] = halves.astype(jnp.bfloat16)

        @pl.loop(1, NQ)
        def _(r):
            q = lax.rem(me_q + r, NQ)
            remote(u_send.at[k, q], ret.at[k, c, me_q], u_sem.at[0, k], u_sem.at[1, k], (q * 2 + c, x)).start()

        ret[k, c, me_q] = u_send[k, me_q]

    finish(0)
    whole.wait_recv()
    sec_in[me_q] = sec_out[me_q]
    grad[1] = sec_in[...].reshape(BLK, BLK)
    finish(1)
    for k in range(2):
        u_whole(k).wait_recv()
        u_core(k).start()
    for k in range(2):
        u_core(k).wait_recv()

    for i in range(12):
        for j in range(6):
            slot = table_s[6 * i + j, 2]
            tile = ret[lax.rem(slot, 2), lax.rem(lax.div(slot, 2), 2), lax.div(slot, 4)].astype(jnp.float32)
            for h in range(2):
                rows = jnp.where(c == 0, tile[8 * h : 8 * h + 4], tile[8 * h + 4 : 8 * h + 8])
                for r in range(4):
                    stage[r, i : i + 1, pl.ds(j * BLK + h * (BLK // 2), BLK // 2)] = rows[r : r + 1]

    update_ref[...] = stage[:, 0:12, :].astype(jnp.bfloat16)
    for k in range(2):
        u_whole(k).wait_send()
        u_core(k).wait_send()
        for n in range(4):
            fresh_out(n, k).wait()

    whole.wait_send()
    sec_copy.wait_send()
    cot_copy.wait_send()
    core_shard(0, 1).wait_send()
    core_shard(3, 2).wait_send()
    core_shard(1, 3).wait_send()
    for p in range(PIECES):
        core_piece(p).wait_send()
        own_piece(p, 0).wait_send()
        own_piece(p, 1).wait_send()
        forward_piece(p, 0 if p < 3 else 1).wait_send()
    for d in range(2):
        for dz in range(NZ):
            hop(ya2_s, ya2_r, ya2_sem, (dz, d), y_target(d)).wait_send()
            hop(ya1_s, ya1_r, ya1_sem, (dz, d), y_target(d)).wait_send()
        hop(za4_s, za4_r, za4_sem, (d,), z_target(d)).wait_send()
        hop(yb2_s, yb2_r, yb2_sem, (d,), y_target(d)).wait_send()
        hop(yb1_s, yb1_r, yb1_sem, (d,), y_target(d)).wait_send()
        for k in range(3):
            hop(za_s, za_r, za_sem, (k, d), z_target(d)).wait_send()
            for dy in range(NY):
                hop(zb_s, zb_r, zb_sem, (k, dy, d), z_target(d)).wait_send()
        for dy in range(NY):
            hop(zb4_s, zb4_r, zb4_sem, (dy, d), z_target(d)).wait_send()


def on_device(
    activations, cotangent, block_owner, left_factor, right_factor, left_basis, right_basis
):
    token_scale = 1.0 / math.sqrt(activations.shape[0] * lax.axis_size("dp"))
    i16, f32, i32, bf16 = jnp.int16, jnp.float32, jnp.int32, jnp.bfloat16
    vmem, dma = pltpu.VMEM, pltpu.SemaphoreType.DMA

    def pair(shape):
        return [vmem(shape, i16), vmem(shape, i16)]

    ha, hb = RA // 2 + 16, RB // 2 + 16
    fa, fb = RA + 16, RB + 16
    whole = pl.BlockSpec(memory_space=pltpu.VMEM)
    anywhere = pl.BlockSpec(memory_space=pl.ANY)
    return pl.pallas_call(
        functools.partial(gradient_kernel, token_scale),
        out_shape=(jax.ShapeDtypeStruct((4, 12, 1536), bf16),)
        + tuple(jax.ShapeDtypeStruct((2, BLK, BLK), f32) for _ in range(4)),
        in_specs=[whole] + [anywhere] * 6,
        out_specs=[whole] + [anywhere] * 4,
        scratch_shapes=[
            vmem((1, 128), i32),
            vmem((512, 768), bf16),
            vmem((4, 2, BLK, BLK), f32),
            vmem((4, 2, BLK, BLK), f32),
            vmem((2, BLK, BLK), f32),
            vmem((2, NQ, 16, BLK // 2), bf16),
            vmem((2, 2, NQ, 16, BLK // 2), bf16),
            vmem((4, 16, 1536), f32),
            vmem((136, 128), i32),
            pltpu.SMEM((136, 128), i32),
            vmem((2, 3 * NX, BLK, 512), bf16),
            vmem((2, 6, 512, BLK), bf16),
            vmem((NZ, NY, RA + RB, BLK), f32),
            vmem((NQ, 8, BLK), f32),
        ]
        + pair((NZ, 2, ha, BLK))
        + pair((NZ, 2, fa, BLK))
        + pair((2, ha, BLK))
        + pair((3, 2, fa, BLK))
        + pair((NY, 2, hb, BLK))
        + pair((3, NY, 2, fb, BLK))
        + pair((2, hb, BLK))
        + pair((2, fb, BLK))
        + [
            vmem((2, SPARE // 2, 8, BLK), f32),
            vmem((NQ, 8, BLK), f32),
            vmem((NQ, 8, BLK), f32),
            dma((2, PIECES)),
            dma((2, PIECES)),
            dma((PIECES,)),
            dma((PIECES,)),
            dma((10,)),
            dma((10,)),
            dma((2, NZ, 2)),
            dma((2, NZ, 2)),
            dma((2, 2)),
            dma((2, 3, 2)),
            dma((2, NY, 2)),
            dma((2, 3, NY, 2)),
            dma((2, 2)),
            dma((2, 2)),
            dma,
            dma((4,)),
            dma((8,)),
            dma((4,)),
            dma((4, 2)),
            dma((2, 2)),
            dma((2, 2)),
        ],
        compiler_params=pltpu.CompilerParams(
            collective_id=0, has_side_effects=True, vmem_limit_bytes=58 * 1024 * 1024
        ),
    )(block_owner.reshape(1, 72), activations, cotangent, left_factor, right_factor, left_basis, right_basis)


def solution(mesh):
    placed = (
        P("dp", "mp"),
        P("dp", "mp"),
        P(),
        P("dp", "mp", None),
        P("dp", "mp", None),
        P("dp", "mp", None),
        P("dp", "mp", None),
    )
    return jax.shard_map(
        on_device,
        mesh=mesh,
        in_specs=placed,
        out_specs=(
            P("dp", None, "mp"),
            P("dp", "mp", None),
            P("dp", "mp", None),
            P("dp", "mp", None),
            P("dp", "mp", None),
        ),
        check_vma=False,
    )
```

```python
import functools
import math

import jax
import jax.numpy as jnp
from jax import lax
from jax.experimental import pallas as pl
from jax.experimental.pallas import tpu as pltpu
from jax.sharding import PartitionSpec as P

NSTEPS = 6
BETA = 0.9
EPS = 1e-06
MESH = pl.DeviceIdType.MESH
NX, NY, NZ, NQ = 4, 4, 8, 32
BLK = 256
SLICES = ((64, 64), (96, 64))
SPARE = 8
PROWS = 128


def place():
    dp = lax.axis_index("dp")
    x = lax.axis_index("mp")
    return x, lax.rem(lax.div(dp, 2), NY), lax.div(dp, 2 * NY), lax.rem(dp, 2)


def device(dx=0, dy=0, dz=0, dc=0):
    x, y, z, c = place()
    x = lax.rem(x + dx + NX, NX)
    y = lax.rem(y + dy + NY, NY)
    z = lax.rem(z + dz + NZ, NZ)
    c = lax.rem(c + dc, 2)
    return ((z * NY + y) * 2 + c, x)


def remote(src, dst, send, recv, target):
    return pltpu.make_async_remote_copy(
        src_ref=src, dst_ref=dst, send_sem=send, recv_sem=recv, device_id=target, device_id_type=MESH
    )


def encode(read, groups, dst):
    exponents = []
    for g in range(groups):
        value = read(g)
        top = jnp.max(jnp.abs(value), axis=0, keepdims=True)
        exponent = jnp.ceil(jnp.log2(jnp.maximum(top, 1e-30) * (1.0 / 32700.0)))
        exponents.append(exponent)
        coded = jnp.round(value * jnp.exp2(-exponent))
        dst[pl.ds(16 * g, 16), :] = coded.astype(jnp.int32).astype(jnp.int16)
    exponents.append(jnp.zeros((16 - groups, BLK), jnp.float32))
    tile = jnp.concatenate(exponents, axis=0)
    dst[pl.ds(16 * groups, 16), :] = tile.astype(jnp.int32).astype(jnp.int16)


def decoder(src, groups):
    scales = jnp.exp2(src[pl.ds(16 * groups, 16), :].astype(jnp.int32).astype(jnp.float32))

    def read(g):
        value = src[pl.ds(16 * g, 16), :].astype(jnp.int32).astype(jnp.float32)
        return value * scales[g : g + 1, :]

    return read


def split(value):
    high = value.astype(jnp.bfloat16)
    return high, (value - high.astype(jnp.float32)).astype(jnp.bfloat16)


def turned(parts):
    return parts[0].T, parts[1].T


def times(left_parts, right_parts):
    def dot(a, b):
        return jnp.dot(a, b, preferred_element_type=jnp.float32)

    low = dot(left_parts[1], right_parts[0]) + dot(left_parts[0], right_parts[1])
    return dot(left_parts[0], right_parts[0]) + low


def refresh(gradient, held, fresh, k, live):
    def keep(n, value):
        fresh[n, k] = value if live is None else jnp.where(live, value, held[n, k])

    g = split(gradient)
    gt = turned(g)
    share = (1.0 - BETA) / BLK
    factors = [BETA * held[0, k] + share * times(g, gt), BETA * held[1, k] + share * times(gt, g)]
    powers, scales = [], []
    for n in range(2):
        keep(n, factors[n])
        power = times(split(factors[n]), split(held[2 + n, k]))
        square = jnp.sum(power * power, axis=0, keepdims=True)
        scales.append(jnp.exp(-0.125 * jnp.log(square * (1.0 / BLK) + EPS)))
        powers.append(power / jnp.sqrt(jnp.sum(square, axis=1, keepdims=True) + EPS))

    def step(_, values):
        parts = [split(v) for v in values]
        grams = [times(turned(p), p) for p in parts]
        moves = [times(p, split(gram)) for p, gram in zip(parts, grams)]
        return tuple(1.5 * v - 0.5 * m for v, m in zip(values, moves))

    bases = lax.fori_loop(0, NSTEPS, step, tuple(powers))
    weights = []
    for n in range(2):
        keep(2 + n, bases[n])
        weights.append(times(split(bases[n] * scales[n]), turned(split(bases[n]))))
    inner = times(g, split(weights[1]))
    return times(split(weights[0]), split(inner))


def gradient_kernel(
    token_scale,
    owner_ref,
    act_hbm,
    cot_hbm,
    left_hbm,
    right_hbm,
    left_basis_hbm,
    right_basis_hbm,
    slots_out,
    ret_out,
    left_out,
    right_out,
    left_basis_out,
    right_basis_out,
    owner_v,
    act_ref,
    held,
    fresh,
    grad,
    u_send,
    ret,
    table_v,
    table_s,
    at,
    cot2,
    spill,
    rings,
    sec,
    sec_out,
    sec_in,
    x_send,
    x_recv,
    f_send,
    f_recv,
    c_send,
    c_recv,
    t_sem,
    s_sem,
    in_sem,
    held_sem,
    out_sem,
    u_sem,
    r_sem,
):
    x, y, z, c = place()
    me_q = z * NY + y
    other = device(dc=1)

    def act_in(n):
        columns = pl.ds(n * 384, 384)
        return pltpu.make_async_copy(act_hbm.at[:, columns], act_ref.at[:, columns], in_sem.at[6 + n])

    def cot_in(j):
        return pltpu.make_async_copy(cot_hbm.at[:, pl.ds(j * BLK, BLK)], cot2.at[0, j], in_sem.at[j])

    factors = (left_hbm, right_hbm, left_basis_hbm, right_basis_hbm)
    results = (left_out, right_out, left_basis_out, right_basis_out)

    def held_in(n):
        return pltpu.make_async_copy(factors[n], held.at[n], held_sem.at[n])

    def fresh_out(n, k):
        return pltpu.make_async_copy(fresh.at[n, k], results[n].at[k], out_sem.at[n, k])

    act_in(0).start()
    act_in(1).start()
    for j in range(6):
        cot_in(j).start()
    for n in range(4):
        held_in(n).start()

    barrier = pltpu.get_barrier_semaphore()
    neighbours = [device(dx=1), device(dx=3), device(dy=1), device(dy=3), device(dz=1), device(dz=7), other]
    for target in neighbours:
        pl.semaphore_signal(barrier, inc=1, device_id=target, device_id_type=MESH)

    def turn(s, p):
        at[s][0, p] = act_ref[:, pl.ds(p * BLK + s * PROWS, PROWS)].T

    def own_piece(s, p, d):
        sgn = 1 - 2 * d
        return remote(
            at[s].at[0, p],
            at[s].at[0, 3 * ((4 - sgn) % 4) + p],
            x_send.at[s, d, p],
            x_recv.at[s, d, p],
            device(dx=sgn),
        )

    far = ((0, 0, 128, 0), (2, 0, 128, 1), (1, 0, 64, 0), (1, 64, 64, 1))

    def forward_piece(s, n):
        p, start, size, d = far[n]
        sgn = 1 - 2 * d
        rows = pl.ds(start, size)
        return remote(
            at[s].at[0, 3 * ((4 - sgn) % 4) + p, rows],
            at[s].at[0, 6 + p, rows],
            f_send.at[s, n],
            f_recv.at[s, n],
            device(dx=sgn),
        )

    def core_shard(s, r):
        rows = pl.ds(3 * r, 3)
        n = {0: 0, 3: 1, 1: 2}[r]
        return remote(at[s].at[0, rows], at[s].at[1, rows], c_send.at[s, n], c_recv.at[s, n], other)

    def core_piece(s, n):
        p, start, size, _ = far[n]
        rows = pl.ds(start, size)
        return remote(
            at[s].at[0, 6 + p, rows], at[s].at[1, 6 + p, rows], c_send.at[s, 3 + n], c_recv.at[s, 3 + n], other
        )

    def gather_start(s):
        for n in range(3):
            own_piece(s, n, 0).start()
            own_piece(s, 2 - n, 1).start()
        core_shard(s, 0).start()

    def gather_forward(s):
        for n in range(4):
            p, _, _, d = far[n]
            own_piece(s, p, d).wait_recv()
            forward_piece(s, n).start()
        own_piece(s, 2, 0).wait_recv()
        own_piece(s, 0, 1).wait_recv()

    def gather_share(s):
        core_shard(s, 3).start()
        core_shard(s, 1).start()

    def gather_end(s):
        for n in range(4):
            forward_piece(s, n).wait_recv()
            core_piece(s, n).start()
        for r in (0, 3, 1):
            core_shard(s, r).wait_recv()
        for n in range(4):
            core_piece(s, n).wait_recv()

    act_in(0).wait()
    act_in(1).wait()
    for p in (0, 2, 1):
        turn(0, p)
    pl.semaphore_wait(barrier, 7)
    gather_start(0)
    for j in range(6):
        cot_in(j).wait()
    cot_copy = remote(cot2.at[0], cot2.at[1], c_send.at[0, 7], c_recv.at[0, 7], other)
    cot_copy.start()
    for p in range(3):
        turn(1, p)

    owner_v[...] = jnp.full((1, 128), -1, jnp.int32)
    owner_v[:, pl.ds(0, 72)] = owner_ref[...]
    owners = owner_v[...]
    lanes = lax.broadcasted_iota(jnp.int32, (128, 128), 1)
    subs = lax.broadcasted_iota(jnp.int32, (128, 128), 0)
    earlier = lanes < subs
    owner_column = jnp.broadcast_to(owners, (128, 128)).T
    same = owner_column == owners
    is_second = jnp.max(jnp.where(same & earlier & (subs < 72), 1, 0), axis=1, keepdims=True)
    is_second = jnp.broadcast_to(is_second, (128, 128))
    second_row = is_second.T
    rank = jnp.sum(jnp.where(earlier, second_row, 0), axis=1, keepdims=True)
    rank = jnp.broadcast_to(rank, (128, 128))
    rank_row = rank.T
    mine = owners == subs
    first = jnp.min(jnp.where(mine, lanes, 71), axis=1, keepdims=True)
    entry = jnp.sum(jnp.where(mine, second_row * rank_row, 0), axis=1, keepdims=True)
    numbers = jnp.sum(jnp.where(rank == lanes, is_second * subs, 0), axis=0, keepdims=True)
    entry = jnp.minimum(entry, SPARE - 1)
    count = jnp.sum(jnp.where(mine, 1, 0), axis=1, keepdims=True)
    columns = jnp.where(lanes == 0, first, jnp.where(lanes == 1, entry, count))
    table_v[0:128, :] = columns
    table_v[128:136, :] = jnp.broadcast_to(numbers, (8, 128))
    slots_out[...] = (2 * owners + second_row[0:1, :])[:, 0:72]
    table_copy = pltpu.make_async_copy(table_v, table_s, t_sem)
    table_copy.start()
    table_copy.wait()

    gather_forward(0)
    gather_start(1)
    gather_share(0)

    def product_of(block, s):
        band = lax.rem(lax.div(block, 6) - 3 * x + 12, 12)
        column = lax.rem(block, 6)
        total = jnp.dot(at[s][0, band], cot2[0, column], preferred_element_type=jnp.float32)
        total += jnp.dot(at[s][1, band], cot2[1, column], preferred_element_type=jnp.float32)
        return total * token_scale

    def ring(s):
        ra, rb = SLICES[s]
        part = rings[s]["part"]
        wire = rings[s]["wire"]
        sems = rings[s]["sems"]

        def hop(name, index, target, rows=None):
            src, dst = wire[name]
            send, recv = sems[name].at[(0,) + index], sems[name].at[(1,) + index]
            if rows is not None:
                index = index + (pl.ds(0, rows),)
            return remote(src.at[index], dst.at[index], send, recv, target)

        def produce(dz):
            @pl.loop(0, NY)
            def _(dy):
                q = lax.rem(z + dz, NZ) * NY + lax.rem(y + dy, NY)
                part[dz, dy, pl.ds(0, PROWS), :] = product_of(table_s[2 * q + c, 0], s)

        def rows_of(dz, dy, start):
            def read(g):
                return part[dz, dy, pl.ds(start + 16 * g, 16), :]

            return read

        def joined(reads, groups):
            def read(g):
                return reads[g // groups](g % groups)

            return read

        def plus(first_read, second_read, low, high, shift=0):
            def read(g):
                if low <= g < high:
                    return first_read(g) + second_read(g - low + shift)
                return first_read(g)

            return read

        ga, gb = ra // 16, rb // 16
        pairs = {4: (4,), 3: (3, 5), 2: (2, 6), 1: (1, 7), 0: (0,)}

        def y_target(d):
            return device(dy=1 - 2 * d)

        def z_target(d):
            return device(dz=1 - 2 * d)

        def a_y2(k):
            rows = len(pairs[k]) * ra // 2 + 16
            for d in range(2):
                reads = [rows_of(dz, 2, d * (ra // 2)) for dz in pairs[k]]
                encode(joined(reads, ga // 2), len(reads) * ga // 2, wire["ya2"][0].at[k, d])
                hop("ya2", (k, d), y_target(d), rows).start()

        def a_y1(k):
            count = len(pairs[k])
            for d in range(2):
                hop("ya2", (k, d), y_target(d), count * ra // 2 + 16).wait_recv()
                arrived = decoder(wire["ya2"][1].at[k, d], count * ga // 2)
                low = d * (ga // 2)
                reads = [
                    plus(rows_of(dz, 1 + 2 * d, 0), arrived, low, low + ga // 2, n * (ga // 2))
                    for n, dz in enumerate(pairs[k])
                ]
                encode(joined(reads, ga), count * ga, wire["ya1"][0].at[k, d])
                hop("ya1", (k, d), y_target(d), count * ra + 16).start()

        def a_yf(k):
            count = len(pairs[k])
            for d in range(2):
                hop("ya1", (k, d), y_target(d), count * ra + 16).wait_recv()
            left, right = [decoder(wire["ya1"][1].at[k, d], count * ga) for d in range(2)]
            for n, dz in enumerate(pairs[k]):
                for g in range(ga):
                    part[dz, 0, pl.ds(16 * g, 16), :] += left(n * ga + g) + right(n * ga + g)

        def a_z(k):
            for d in range(2):
                dz = k if d == 0 else 8 - k
                if k == 4:
                    encode(rows_of(4, 0, d * (ra // 2)), ga // 2, wire["za4"][0].at[d])
                    hop("za4", (d,), z_target(d)).start()
                    continue
                if k == 3:
                    hop("za4", (d,), z_target(d)).wait_recv()
                    low = d * (ga // 2)
                    read = plus(rows_of(dz, 0, 0), decoder(wire["za4"][1].at[d], ga // 2), low, low + ga // 2)
                else:
                    hop("za", (k, d), z_target(d)).wait_recv()
                    read = plus(rows_of(dz, 0, 0), decoder(wire["za"][1].at[k, d], ga), 0, ga)
                encode(read, ga, wire["za"][0].at[k - 1, d])
                hop("za", (k - 1, d), z_target(d)).start()

        def b_z(k):
            @pl.loop(0, 2)
            def _(n):
                for d in range(2):
                    dz = k if d == 0 else 8 - k
                    dys = (2 - 2 * n, 3 - 2 * n)
                    if k == 4:
                        reads = [rows_of(4, dy, ra + d * (rb // 2)) for dy in dys]
                        encode(joined(reads, gb // 2), gb, wire["zb4"][0].at[n, d])
                        hop("zb4", (n, d), z_target(d)).start()
                        continue
                    if k == 3:
                        hop("zb4", (n, d), z_target(d)).wait_recv()
                        arrived = decoder(wire["zb4"][1].at[n, d], gb)
                        low, many = d * (gb // 2), gb // 2
                    else:
                        hop("zb", (k, n, d), z_target(d)).wait_recv()
                        arrived = decoder(wire["zb"][1].at[k, n, d], 2 * gb)
                        low, many = 0, gb
                    reads = [
                        plus(rows_of(dz, dy, ra), arrived, low, low + many, m * many) for m, dy in enumerate(dys)
                    ]
                    encode(joined(reads, gb), 2 * gb, wire["zb"][0].at[k - 1, n, d])
                    hop("zb", (k - 1, n, d), z_target(d)).start()

        def b_zf(n):
            for d in range(2):
                hop("zb", (0, n, d), z_target(d)).wait_recv()
            left, right = [decoder(wire["zb"][1].at[0, n, d], 2 * gb) for d in range(2)]
            for m in range(2):
                for g in range(gb):
                    part[0, 2 - 2 * n + m, pl.ds(ra + 16 * g, 16), :] += left(m * gb + g) + right(m * gb + g)

        def b_y2():
            for d in range(2):
                encode(rows_of(0, 2, ra + d * (rb // 2)), gb // 2, wire["yb2"][0].at[d])
                hop("yb2", (d,), y_target(d)).start()

        def b_y1():
            for d in range(2):
                hop("yb2", (d,), y_target(d)).wait_recv()
                low = d * (gb // 2)
                arrived = decoder(wire["yb2"][1].at[d], gb // 2)
                encode(plus(rows_of(0, 1 + 2 * d, ra), arrived, low, low + gb // 2), gb, wire["yb1"][0].at[d])
                hop("yb1", (d,), y_target(d)).start()

        def finish_b(store):
            for d in range(2):
                hop("yb1", (d,), y_target(d)).wait_recv()
            left, right = [decoder(wire["yb1"][1].at[d], gb) for d in range(2)]
            for g in range(gb):
                store(g, part[0, 0, pl.ds(ra + 16 * g, 16), :] + left(g) + right(g))

        def finish_a(store):
            for d in range(2):
                hop("za", (0, d), z_target(d)).wait_recv()
            left, right = [decoder(wire["za"][1].at[0, d], ga) for d in range(2)]
            for g in range(ga):
                store(g, part[0, 0, pl.ds(16 * g, 16), :] + left(g) + right(g))

        def phase(n):
            if n == 0:
                produce(4)
                b_z(4)
                a_y2(4)
            elif n == 1:
                produce(3)
                produce(5)
                a_y2(3)
                b_z(3)
                a_y1(4)
            elif n == 2:
                produce(2)
                produce(6)
                a_y2(2)
                a_y1(3)
                b_z(2)
                a_yf(4)
                a_z(4)
            elif n == 3:
                produce(1)
                produce(7)
                a_y2(1)
                a_y1(2)
                a_yf(3)
                a_z(3)
                b_z(1)
            elif n == 4:
                produce(0)
                a_y2(0)
                a_y1(1)
                a_yf(2)
                a_z(2)
                b_zf(0)
                b_y2()
            elif n == 5:
                a_y1(0)
                a_yf(1)
                a_z(1)
                b_zf(1)
                b_y1()
                a_yf(0)

        def drain():
            for d in range(2):
                for k in range(5):
                    hop("ya2", (k, d), y_target(d), len(pairs[k]) * ra // 2 + 16).wait_send()
                    hop("ya1", (k, d), y_target(d), len(pairs[k]) * ra + 16).wait_send()
                hop("za4", (d,), z_target(d)).wait_send()
                hop("yb2", (d,), y_target(d)).wait_send()
                hop("yb1", (d,), y_target(d)).wait_send()
                for k in range(3):
                    hop("za", (k, d), z_target(d)).wait_send()
                    for n in range(2):
                        hop("zb", (k, n, d), z_target(d)).wait_send()
                for n in range(2):
                    hop("zb4", (n, d), z_target(d)).wait_send()

        return phase, finish_a, finish_b, drain

    phase1, finish_a1, finish_b1, drain1 = ring(0)
    phase2, finish_a2, finish_b2, drain2 = ring(1)

    def second_rows(h):
        ra = SLICES[1][0]

        @pl.loop(0, SPARE // 2)
        def _(s):
            spill[...] = product_of(table_s[128, 2 * s + c], h).reshape(NQ // 2, 8, BLK)

            @pl.loop(0, NQ // 2)
            def _(r):
                q = r + h * (NQ // 2)
                dz = lax.rem(lax.div(q, NY) - z + NZ, NZ)
                dy = lax.rem(lax.rem(q, NY) - y + NY, NY)
                rings[1]["part"][dz, dy, pl.ds(pl.multiple_of(PROWS + 8 * s, 8), 8), :] = spill[r]

    def store_a1(g, rows):
        grad[0, pl.ds(16 * g, 16), :] = rows

    def store_b1(g, rows):
        grad[0, pl.ds(64 + 16 * g, 16), :] = rows

    def store_a2(g, rows):
        grad[0, pl.ds(PROWS + 16 * g, 16), :] = rows

    def store_b2(g, rows):
        if g < 2:
            grad[0, pl.ds(224 + 16 * g, 16), :] = rows
        else:
            sec[c, pl.ds(2 * (g - 2), 2)] = rows.reshape(2, 8, BLK)

    gather_end(0)
    cot_copy.wait_recv()
    phase1(0)
    phase1(1)
    second_rows(0)
    gather_forward(1)
    gather_share(1)
    phase1(2)
    phase1(3)
    gather_end(1)
    second_rows(1)
    phase2(0)
    phase1(4)
    phase2(1)
    phase1(5)
    phase2(2)
    finish_b1(store_b1)
    finish_a1(store_a1)
    phase2(3)
    phase2(4)
    phase2(5)
    finish_b2(store_b2)
    sec_copy = remote(sec.at[c], sec.at[c], s_sem.at[0], s_sem.at[1], other)
    sec_copy.start()

    finish_a2(store_a2)

    sec_copy.wait_recv()

    @pl.loop(0, NQ)
    def _(q):
        place_of = table_s[2 * q + c, 1]
        sec_out[q] = sec[lax.rem(place_of, 2), lax.div(place_of, 2)]

    @pl.loop(1, NQ)
    def _(r):
        q = lax.rem(me_q + r, NQ)
        remote(sec_out.at[q], sec_in.at[me_q], s_sem.at[2], s_sem.at[3], (q * 2 + c, x)).start()

    whole = remote(sec_out.at[pl.ds(0, NQ - 1)], sec_in.at[pl.ds(0, NQ - 1)], s_sem.at[2], s_sem.at[3], other)
    for n in range(4):
        held_in(n).wait()

    def u_whole(k):
        part_of = pl.ds(0, NQ - 1)
        return remote(u_send.at[k, part_of], ret.at[k, c, part_of], u_sem.at[0, k], u_sem.at[1, k], other)

    def u_core(k):
        return remote(ret.at[k, c], ret.at[k, c], r_sem.at[0, k], r_sem.at[1, k], other)

    def finish(k):
        update = refresh(grad[k], held, fresh, k, None if k == 0 else table_s[me_q * 2 + c, 2] > 1)
        for n in range(4):
            fresh_out(n, k).start()
        rows = update.reshape(NQ, 8, BLK)
        halves = jnp.concatenate([rows[:, :, : BLK // 2], rows[:, :, BLK // 2 :]], axis=1)
        u_send[k] = halves.astype(jnp.bfloat16)

        @pl.loop(1, NQ)
        def _(r):
            q = lax.rem(me_q + r, NQ)
            remote(u_send.at[k, q], ret.at[k, c, me_q], u_sem.at[0, k], u_sem.at[1, k], (q * 2 + c, x)).start()

        ret[k, c, me_q] = u_send[k, me_q]

    finish(0)
    whole.wait_recv()
    sec_in[me_q] = sec_out[me_q]
    grad[1] = sec_in[...].reshape(BLK, BLK)
    finish(1)
    for k in range(2):
        u_whole(k).wait_recv()
        u_core(k).start()
    for k in range(2):
        u_core(k).wait_recv()

    ret_copy = pltpu.make_async_copy(ret, ret_out, t_sem)
    ret_copy.start()
    for k in range(2):
        u_whole(k).wait_send()
        u_core(k).wait_send()
        for n in range(4):
            fresh_out(n, k).wait()

    whole.wait_send()
    sec_copy.wait_send()
    cot_copy.wait_send()
    for s in range(2):
        for r in (0, 3, 1):
            core_shard(s, r).wait_send()
        for n in range(4):
            core_piece(s, n).wait_send()
            forward_piece(s, n).wait_send()
        for p in range(3):
            own_piece(s, p, 0).wait_send()
            own_piece(s, p, 1).wait_send()
    drain1()
    drain2()
    ret_copy.wait()


def hand_over(slots, returned, results):
    def body(slot_ref, ret_hbm, *refs):
        sources, update_ref, targets = refs[:4], refs[4], refs[5:9]
        ret, held, in_sem, out_sem = refs[9:]
        core = lax.rem(lax.axis_index("dp"), 2)
        loads = [pltpu.make_async_copy(sources[n], held.at[n], in_sem.at[n]) for n in range(4)]
        stores = [pltpu.make_async_copy(held.at[n], targets[n], out_sem.at[n]) for n in range(4)]
        rows_in = pltpu.make_async_copy(ret_hbm, ret, in_sem.at[4])
        rows_in.start()
        for load in loads:
            load.start()
        for load, store in zip(loads, stores):
            load.wait()
            store.start()
        rows_in.wait()
        for i in range(12):
            for j in range(6):
                slot = slot_ref[0, 6 * i + j]
                tile = ret[lax.rem(slot, 2), lax.rem(lax.div(slot, 2), 2), lax.div(slot, 4)].astype(jnp.float32)
                for h in range(2):
                    rows = jnp.where(core == 0, tile[8 * h : 8 * h + 4], tile[8 * h + 4 : 8 * h + 8])
                    columns = pl.ds(j * BLK + h * (BLK // 2), BLK // 2)
                    update_ref[i, :, columns] = rows.astype(jnp.bfloat16)
        for store in stores:
            store.wait()

    anywhere = pl.BlockSpec(memory_space=pl.ANY)
    return pl.pallas_call(
        body,
        out_shape=(jax.ShapeDtypeStruct((12, 4, 1536), jnp.bfloat16),)
        + tuple(jax.ShapeDtypeStruct(r.shape, r.dtype) for r in results),
        in_specs=[pl.BlockSpec(memory_space=pltpu.SMEM)] + [anywhere] * 5,
        out_specs=[pl.BlockSpec(memory_space=pltpu.VMEM)] + [anywhere] * 4,
        scratch_shapes=[
            pltpu.VMEM(returned.shape, returned.dtype),
            pltpu.VMEM((4, 2, BLK, BLK), jnp.float32),
            pltpu.SemaphoreType.DMA((5,)),
            pltpu.SemaphoreType.DMA((4,)),
        ],
    )(slots, returned, *results)


def on_device(
    activations, cotangent, block_owner, left_factor, right_factor, left_basis, right_basis
):
    token_scale = 1.0 / math.sqrt(activations.shape[0] * lax.axis_size("dp"))
    i16, f32, i32, bf16 = jnp.int16, jnp.float32, jnp.int32, jnp.bfloat16
    vmem, dma = pltpu.VMEM, pltpu.SemaphoreType.DMA

    def pair(*shape):
        return (vmem(shape + (BLK,), i16), vmem(shape + (BLK,), i16))

    def ring_scratch(ra, rb):
        return dict(
            part=vmem((NZ, NY, ra + rb, BLK), f32),
            wire=dict(
                ya2=pair(5, 2, ra + 16),
                ya1=pair(5, 2, 2 * ra + 16),
                za4=pair(2, ra // 2 + 16),
                za=pair(3, 2, ra + 16),
                zb4=pair(2, 2, rb + 16),
                zb=pair(3, 2, 2, 2 * rb + 16),
                yb2=pair(2, rb // 2 + 16),
                yb1=pair(2, rb + 16),
            ),
            sems=dict(
                ya2=dma((2, 5, 2)),
                ya1=dma((2, 5, 2)),
                za4=dma((2, 2)),
                za=dma((2, 3, 2)),
                zb4=dma((2, 2, 2)),
                zb=dma((2, 3, 2, 2)),
                yb2=dma((2, 2)),
                yb1=dma((2, 2)),
            ),
        )

    whole = pl.BlockSpec(memory_space=pltpu.VMEM)
    anywhere = pl.BlockSpec(memory_space=pl.ANY)
    slots, returned, *results = pl.pallas_call(
        functools.partial(gradient_kernel, token_scale),
        out_shape=(jax.ShapeDtypeStruct((1, 72), i32), jax.ShapeDtypeStruct((2, 2, NQ, 16, BLK // 2), bf16))
        + tuple(jax.ShapeDtypeStruct((2, BLK, BLK), f32) for _ in range(4)),
        in_specs=[whole] + [anywhere] * 6,
        out_specs=[whole] + [anywhere] * 5,
        scratch_shapes=[
            vmem((1, 128), i32),
            vmem((512, 768), bf16),
            vmem((4, 2, BLK, BLK), f32),
            vmem((4, 2, BLK, BLK), f32),
            vmem((2, BLK, BLK), f32),
            vmem((2, NQ, 16, BLK // 2), bf16),
            vmem((2, 2, NQ, 16, BLK // 2), bf16),
            vmem((136, 128), i32),
            pltpu.SMEM((136, 128), i32),
            tuple(vmem((2, 3 * NX, PROWS, 512), bf16) for _ in SLICES),
            vmem((2, 6, 512, BLK), bf16),
            vmem((NQ // 2, 8, BLK), f32),
            tuple(ring_scratch(*rows) for rows in SLICES),
            vmem((2, SPARE // 2, 8, BLK), f32),
            vmem((NQ, 8, BLK), f32),
            vmem((NQ, 8, BLK), f32),
            dma((2, 2, 3)),
            dma((2, 2, 3)),
            dma((2, 4)),
            dma((2, 4)),
            dma((2, 8)),
            dma((2, 8)),
            dma,
            dma((4,)),
            dma((8,)),
            dma((4,)),
            dma((4, 2)),
            dma((2, 2)),
            dma((2, 2)),
        ],
        compiler_params=pltpu.CompilerParams(
            collective_id=0, has_side_effects=True, vmem_limit_bytes=58 * 1024 * 1024
        ),
    )(block_owner.reshape(1, 72), activations, cotangent, left_factor, right_factor, left_basis, right_basis)
    update, *results = hand_over(slots, returned, results)
    return (jnp.swapaxes(update, 0, 1), *results)


def solution(mesh):
    placed = (
        P("dp", "mp"),
        P("dp", "mp"),
        P(),
        P("dp", "mp", None),
        P("dp", "mp", None),
        P("dp", "mp", None),
        P("dp", "mp", None),
    )
    return jax.shard_map(
        on_device,
        mesh=mesh,
        in_specs=placed,
        out_specs=(
            P("dp", None, "mp"),
            P("dp", "mp", None),
            P("dp", "mp", None),
            P("dp", "mp", None),
            P("dp", "mp", None),
        ),
        check_vma=False,
    )
```

```python
import functools
import math

import jax
import jax.numpy as jnp
from jax import lax
from jax.experimental import pallas as pl
from jax.experimental.pallas import tpu as pltpu
from jax.sharding import PartitionSpec as P

NSTEPS = 6
BETA = 0.9
EPS = 1e-06
MESH = pl.DeviceIdType.MESH
NX, NY, NZ, NQ = 4, 4, 8, 32
BLK = 256
SLICES = ((64, 64), (96, 64))
SPARE = 8
PROWS = 128
ORDER = (
    ("gf", 0, 1),
    ("gf", 0, 0),
    ("gf", 0, 2),
    ("gf", 0, 3),
    ("gs", 1),
    ("gsh", 0),
    ("ge", 0, 1),
    ("ge", 0, 0),
    ("ge", 0, 2),
    ("ge", 0, 3),
    ("gd", 0),
    ("sec", 0),
    ("P", 0, 4),
    ("gf", 1, 0),
    ("gf", 1, 1),
    ("AY2", 0, 4, 0),
    ("B", 0, 4, 0, 1),
    ("B", 0, 4, 1, 1),
    ("B", 0, 4, 0, 0),
    ("B", 0, 4, 1, 0),
    ("AY2", 0, 4, 1),
    ("P", 0, 5),
    ("gf", 1, 2),
    ("gf", 1, 3),
    ("P", 0, 3),
    ("AY2", 0, 3, 1),
    ("AY1", 0, 4, 0),
    ("AY2", 0, 3, 0),
    ("P", 0, 2),
    ("B", 0, 3, 0, 1),
    ("B", 0, 3, 0, 0),
    ("gsh", 1),
    ("B", 0, 3, 1, 0),
    ("AY1", 0, 4, 1),
    ("B", 0, 3, 1, 1),
    ("P", 0, 7),
    ("P", 0, 1),
    ("AY1", 0, 3, 1),
    ("ge", 1, 1),
    ("ge", 1, 0),
    ("AY1", 0, 3, 0),
    ("AY2", 0, 1, 0),
    ("AY2", 0, 1, 1),
    ("P", 0, 6),
    ("ge", 1, 3),
    ("ge", 1, 2),
    ("B", 0, 2, 0, 0),
    ("B", 0, 2, 0, 1),
    ("AY2", 0, 2, 1),
    ("AY2", 0, 2, 0),
    ("AYF", 0, 4),
    ("AZ", 0, 4, 1),
    ("B", 0, 2, 1, 1),
    ("AZ", 0, 4, 0),
    ("gd", 1),
    ("sec", 1),
    ("P", 1, 4),
    ("AY2", 1, 4, 0),
    ("B", 1, 4, 0, 1),
    ("B", 1, 4, 0, 0),
    ("B", 1, 4, 1, 1),
    ("AY2", 1, 4, 1),
    ("B", 1, 4, 1, 0),
    ("AY1", 0, 2, 0),
    ("B", 0, 1, 0, 1),
    ("B", 0, 2, 1, 0),
    ("P", 1, 3),
    ("AY1", 0, 2, 1),
    ("P", 1, 5),
    ("AY2", 1, 3, 0),
    ("B", 1, 3, 0, 0),
    ("AY1", 1, 4, 0),
    ("AY2", 1, 3, 1),
    ("AY1", 1, 4, 1),
    ("B", 1, 3, 0, 1),
    ("B", 1, 3, 1, 0),
    ("B", 1, 3, 1, 1),
    ("AYF", 0, 3),
    ("AZ", 0, 3, 1),
    ("B", 0, 1, 0, 0),
    ("AZ", 0, 3, 0),
    ("AY1", 0, 1, 1),
    ("P", 1, 6),
    ("B", 0, 1, 1, 0),
    ("P", 1, 2),
    ("AY1", 1, 3, 0),
    ("AY2", 1, 2, 1),
    ("AY2", 1, 2, 0),
    ("AY1", 1, 3, 1),
    ("B", 1, 2, 0, 1),
    ("B", 1, 2, 0, 0),
    ("AYF", 1, 4),
    ("AZ", 1, 4, 1),
    ("AZ", 1, 4, 0),
    ("B", 1, 2, 1, 0),
    ("AY1", 0, 1, 0),
    ("B", 0, 1, 1, 1),
    ("B", 1, 2, 1, 1),
    ("AYF", 0, 2),
    ("P", 1, 7),
    ("AZ", 0, 2, 1),
    ("P", 1, 1),
    ("AY1", 1, 2, 1),
    ("AY2", 1, 1, 1),
    ("AY2", 1, 1, 0),
    ("B", 1, 1, 0, 1),
    ("AZ", 0, 2, 0),
    ("P", 0, 0),
    ("AY1", 1, 2, 0),
    ("AYF", 1, 3),
    ("B", 1, 1, 0, 0),
    ("AZ", 1, 3, 1),
    ("AY2", 0, 0, 1),
    ("AY2", 0, 0, 0),
    ("BF", 0, 0),
    ("AZ", 1, 3, 0),
    ("BY2", 0, 0),
    ("AYF", 0, 1),
    ("BY2", 0, 1),
    ("BF", 0, 1),
    ("P", 1, 0),
    ("B", 1, 1, 1, 0),
    ("AY2", 1, 0, 1),
    ("AY2", 1, 0, 0),
    ("B", 1, 1, 1, 1),
    ("AY1", 1, 1, 0),
    ("AZ", 0, 1, 1),
    ("AZ", 0, 1, 0),
    ("AY1", 1, 1, 1),
    ("AY1", 0, 0, 1),
    ("AYF", 1, 2),
    ("BF", 1, 0),
    ("BY2", 1, 0),
    ("BY2", 1, 1),
    ("BY1", 0, 1),
    ("AY1", 0, 0, 0),
    ("AZ", 1, 2, 1),
    ("BY1", 0, 0),
    ("AZ", 1, 2, 0),
    ("AY1", 1, 0, 1),
    ("AY1", 1, 0, 0),
    ("BF", 1, 1),
    ("AYF", 1, 1),
    ("BY1", 1, 0),
    ("AZ", 1, 1, 1),
    ("AZ", 1, 1, 0),
    ("AYF", 0, 0),
    ("FA", 0),
    ("BY1", 1, 1),
    ("FB", 0),
    ("AYF", 1, 0),
    ("FA", 1),
    ("FB", 1),
)


def place():
    dp = lax.axis_index("dp")
    x = lax.axis_index("mp")
    return x, lax.rem(lax.div(dp, 2), NY), lax.div(dp, 2 * NY), lax.rem(dp, 2)


def device(dx=0, dy=0, dz=0, dc=0):
    x, y, z, c = place()
    x = lax.rem(x + dx + NX, NX)
    y = lax.rem(y + dy + NY, NY)
    z = lax.rem(z + dz + NZ, NZ)
    c = lax.rem(c + dc, 2)
    return ((z * NY + y) * 2 + c, x)


def remote(src, dst, send, recv, target):
    return pltpu.make_async_remote_copy(
        src_ref=src, dst_ref=dst, send_sem=send, recv_sem=recv, device_id=target, device_id_type=MESH
    )


def encode(read, groups, dst):
    exponents = []
    for g in range(groups):
        value = read(g)
        top = jnp.max(jnp.abs(value), axis=0, keepdims=True)
        exponent = jnp.ceil(jnp.log2(jnp.maximum(top, 1e-30) * (1.0 / 32700.0)))
        exponents.append(exponent)
        coded = jnp.round(value * jnp.exp2(-exponent))
        dst[pl.ds(16 * g, 16), :] = coded.astype(jnp.int32).astype(jnp.int16)
    exponents.append(jnp.zeros((16 - groups, BLK), jnp.float32))
    tile = jnp.concatenate(exponents, axis=0)
    dst[pl.ds(16 * groups, 16), :] = tile.astype(jnp.int32).astype(jnp.int16)


def decoder(src, groups):
    scales = jnp.exp2(src[pl.ds(16 * groups, 16), :].astype(jnp.int32).astype(jnp.float32))

    def read(g):
        value = src[pl.ds(16 * g, 16), :].astype(jnp.int32).astype(jnp.float32)
        return value * scales[g : g + 1, :]

    return read


def split(value):
    high = value.astype(jnp.bfloat16)
    return high, (value - high.astype(jnp.float32)).astype(jnp.bfloat16)


def turned(parts):
    return parts[0].T, parts[1].T


def times(left_parts, right_parts):
    def dot(a, b):
        return jnp.dot(a, b, preferred_element_type=jnp.float32)

    both = dot(jnp.concatenate(left_parts, axis=0), right_parts[0])
    return both[:BLK] + (both[BLK:] + dot(left_parts[0], right_parts[1]))


def refresh(gradient, held, fresh, k, live):
    def keep(n, value):
        fresh[n, k] = value if live is None else jnp.where(live, value, held[n, k])

    g = split(gradient)
    gt = turned(g)
    share = (1.0 - BETA) / BLK
    factors = [BETA * held[0, k] + share * times(g, gt), BETA * held[1, k] + share * times(gt, g)]
    powers, scales = [], []
    for n in range(2):
        keep(n, factors[n])
        power = times(split(factors[n]), split(held[2 + n, k]))
        square = jnp.sum(power * power, axis=0, keepdims=True)
        scales.append(jnp.exp(-0.125 * jnp.log(square * (1.0 / BLK) + EPS)))
        powers.append(power / jnp.sqrt(jnp.sum(square, axis=1, keepdims=True) + EPS))

    def step(_, values):
        parts = [split(v) for v in values]
        grams = [times(turned(p), p) for p in parts]
        moves = [times(p, split(gram)) for p, gram in zip(parts, grams)]
        return tuple(1.5 * v - 0.5 * m for v, m in zip(values, moves))

    bases = lax.fori_loop(0, NSTEPS, step, tuple(powers))
    weights = []
    for n in range(2):
        keep(2 + n, bases[n])
        weights.append(times(split(bases[n] * scales[n]), turned(split(bases[n]))))
    inner = times(g, split(weights[1]))
    return times(split(weights[0]), split(inner))


def gradient_kernel(
    token_scale,
    owner_ref,
    act_hbm,
    cot_hbm,
    left_hbm,
    right_hbm,
    left_basis_hbm,
    right_basis_hbm,
    slots_out,
    ret_out,
    left_out,
    right_out,
    left_basis_out,
    right_basis_out,
    owner_v,
    act_ref,
    held,
    fresh,
    grad,
    u_send,
    ret,
    table_v,
    table_s,
    at,
    cot2,
    spill,
    rings,
    sec,
    sec_out,
    sec_in,
    x_send,
    x_recv,
    f_send,
    f_recv,
    c_send,
    c_recv,
    t_sem,
    s_sem,
    in_sem,
    held_sem,
    out_sem,
    u_sem,
    r_sem,
):
    x, y, z, c = place()
    me_q = z * NY + y
    other = device(dc=1)

    def act_in(n):
        columns = pl.ds(n * 384, 384)
        return pltpu.make_async_copy(act_hbm.at[:, columns], act_ref.at[:, columns], in_sem.at[6 + n])

    def cot_in(j):
        return pltpu.make_async_copy(cot_hbm.at[:, pl.ds(j * BLK, BLK)], cot2.at[0, j], in_sem.at[j])

    factors = (left_hbm, right_hbm, left_basis_hbm, right_basis_hbm)
    results = (left_out, right_out, left_basis_out, right_basis_out)

    def held_in(n):
        return pltpu.make_async_copy(factors[n], held.at[n], held_sem.at[n])

    def fresh_out(n, k):
        return pltpu.make_async_copy(fresh.at[n, k], results[n].at[k], out_sem.at[n, k])

    act_in(0).start()
    act_in(1).start()
    for j in range(6):
        cot_in(j).start()
    for n in range(4):
        held_in(n).start()

    barrier = pltpu.get_barrier_semaphore()
    neighbours = [device(dx=1), device(dx=3), device(dy=1), device(dy=3), device(dz=1), device(dz=7), other]
    for target in neighbours:
        pl.semaphore_signal(barrier, inc=1, device_id=target, device_id_type=MESH)

    def turn(s, p):
        at[s][0, p] = act_ref[:, pl.ds(p * BLK + s * PROWS, PROWS)].T

    def own_piece(s, p, d):
        sgn = 1 - 2 * d
        return remote(
            at[s].at[0, p],
            at[s].at[0, 3 * ((4 - sgn) % 4) + p],
            x_send.at[s, d, p],
            x_recv.at[s, d, p],
            device(dx=sgn),
        )

    far = ((0, 0, 128, 0), (2, 0, 128, 1), (1, 0, 64, 0), (1, 64, 64, 1))

    def forward_piece(s, n):
        p, start, size, d = far[n]
        sgn = 1 - 2 * d
        rows = pl.ds(start, size)
        return remote(
            at[s].at[0, 3 * ((4 - sgn) % 4) + p, rows],
            at[s].at[0, 6 + p, rows],
            f_send.at[s, n],
            f_recv.at[s, n],
            device(dx=sgn),
        )

    def core_shard(s, r):
        rows = pl.ds(3 * r, 3)
        n = {0: 0, 3: 1, 1: 2}[r]
        return remote(at[s].at[0, rows], at[s].at[1, rows], c_send.at[s, n], c_recv.at[s, n], other)

    def core_piece(s, n):
        p, start, size, _ = far[n]
        rows = pl.ds(start, size)
        return remote(
            at[s].at[0, 6 + p, rows], at[s].at[1, 6 + p, rows], c_send.at[s, 3 + n], c_recv.at[s, 3 + n], other
        )

    def gather_start(s):
        for n in range(3):
            own_piece(s, n, 0).start()
            own_piece(s, 2 - n, 1).start()
        core_shard(s, 0).start()

    def forward(s, n):
        p, _, _, d = far[n]
        own_piece(s, p, d).wait_recv()
        forward_piece(s, n).start()

    def share(s):
        own_piece(s, 2, 0).wait_recv()
        own_piece(s, 0, 1).wait_recv()
        core_shard(s, 3).start()
        core_shard(s, 1).start()

    def pass_on(s, n):
        forward_piece(s, n).wait_recv()
        core_piece(s, n).start()

    def gathered(s):
        for r in (0, 3, 1):
            core_shard(s, r).wait_recv()
        for n in range(4):
            core_piece(s, n).wait_recv()
        if s == 0:
            cot_copy.wait_recv()

    act_in(0).wait()
    act_in(1).wait()
    for p in (0, 2, 1):
        turn(0, p)
    pl.semaphore_wait(barrier, 7)
    gather_start(0)
    for j in range(6):
        cot_in(j).wait()
    cot_copy = remote(cot2.at[0], cot2.at[1], c_send.at[0, 7], c_recv.at[0, 7], other)
    cot_copy.start()
    for p in range(3):
        turn(1, p)

    owner_v[...] = jnp.full((1, 128), -1, jnp.int32)
    owner_v[:, pl.ds(0, 72)] = owner_ref[...]
    owners = owner_v[...]
    lanes = lax.broadcasted_iota(jnp.int32, (128, 128), 1)
    subs = lax.broadcasted_iota(jnp.int32, (128, 128), 0)
    earlier = lanes < subs
    owner_column = jnp.broadcast_to(owners, (128, 128)).T
    same = owner_column == owners
    is_second = jnp.max(jnp.where(same & earlier & (subs < 72), 1, 0), axis=1, keepdims=True)
    is_second = jnp.broadcast_to(is_second, (128, 128))
    second_row = is_second.T
    rank = jnp.sum(jnp.where(earlier, second_row, 0), axis=1, keepdims=True)
    rank = jnp.broadcast_to(rank, (128, 128))
    rank_row = rank.T
    mine = owners == subs
    first = jnp.min(jnp.where(mine, lanes, 71), axis=1, keepdims=True)
    entry = jnp.sum(jnp.where(mine, second_row * rank_row, 0), axis=1, keepdims=True)
    numbers = jnp.sum(jnp.where(rank == lanes, is_second * subs, 0), axis=0, keepdims=True)
    entry = jnp.minimum(entry, SPARE - 1)
    count = jnp.sum(jnp.where(mine, 1, 0), axis=1, keepdims=True)
    columns = jnp.where(lanes == 0, first, jnp.where(lanes == 1, entry, count))
    table_v[0:128, :] = columns
    table_v[128:136, :] = jnp.broadcast_to(numbers, (8, 128))
    slots_out[...] = (2 * owners + second_row[0:1, :])[:, 0:72]
    table_copy = pltpu.make_async_copy(table_v, table_s, t_sem)
    table_copy.start()
    table_copy.wait()

    def product_of(block, s):
        band = lax.rem(lax.div(block, 6) - 3 * x + 12, 12)
        column = lax.rem(block, 6)
        total = jnp.dot(at[s][0, band], cot2[0, column], preferred_element_type=jnp.float32)
        total += jnp.dot(at[s][1, band], cot2[1, column], preferred_element_type=jnp.float32)
        return total * token_scale

    def ring(s):
        ra, rb = SLICES[s]
        part = rings[s]["part"]
        wire = rings[s]["wire"]
        sems = rings[s]["sems"]

        def hop(name, index, target, rows=None):
            src, dst = wire[name]
            send, recv = sems[name].at[(0,) + index], sems[name].at[(1,) + index]
            if rows is not None:
                index = index + (pl.ds(0, rows),)
            return remote(src.at[index], dst.at[index], send, recv, target)

        def produce(dz):
            @pl.loop(0, NY)
            def _(dy):
                q = lax.rem(z + dz, NZ) * NY + lax.rem(y + dy, NY)
                part[dz, dy, pl.ds(0, PROWS), :] = product_of(table_s[2 * q + c, 0], s)

        def rows_of(dz, dy, start):
            def read(g):
                return part[dz, dy, pl.ds(start + 16 * g, 16), :]

            return read

        def joined(reads, groups):
            def read(g):
                return reads[g // groups](g % groups)

            return read

        def plus(first_read, second_read, low, high, shift=0):
            def read(g):
                if low <= g < high:
                    return first_read(g) + second_read(g - low + shift)
                return first_read(g)

            return read

        ga, gb = ra // 16, rb // 16
        pairs = {4: (4,), 3: (3, 5), 2: (2, 6), 1: (1, 7), 0: (0,)}

        def y_target(d):
            return device(dy=1 - 2 * d)

        def z_target(d):
            return device(dz=1 - 2 * d)

        def a_y2(k, d):
            rows = len(pairs[k]) * ra // 2 + 16
            reads = [rows_of(dz, 2, d * (ra // 2)) for dz in pairs[k]]
            encode(joined(reads, ga // 2), len(reads) * ga // 2, wire["ya2"][0].at[k, d])
            hop("ya2", (k, d), y_target(d), rows).start()

        def a_y1(k, d):
            count = len(pairs[k])
            hop("ya2", (k, d), y_target(d), count * ra // 2 + 16).wait_recv()
            arrived = decoder(wire["ya2"][1].at[k, d], count * ga // 2)
            low = d * (ga // 2)
            reads = [
                plus(rows_of(dz, 1 + 2 * d, 0), arrived, low, low + ga // 2, n * (ga // 2))
                for n, dz in enumerate(pairs[k])
            ]
            encode(joined(reads, ga), count * ga, wire["ya1"][0].at[k, d])
            hop("ya1", (k, d), y_target(d), count * ra + 16).start()

        def a_yf(k):
            count = len(pairs[k])
            for d in range(2):
                hop("ya1", (k, d), y_target(d), count * ra + 16).wait_recv()
            left, right = [decoder(wire["ya1"][1].at[k, d], count * ga) for d in range(2)]
            for n, dz in enumerate(pairs[k]):
                for g in range(ga):
                    part[dz, 0, pl.ds(16 * g, 16), :] += left(n * ga + g) + right(n * ga + g)

        def a_z(k, d):
            dz = k if d == 0 else 8 - k
            if k == 4:
                encode(rows_of(4, 0, d * (ra // 2)), ga // 2, wire["za4"][0].at[d])
                hop("za4", (d,), z_target(d)).start()
                return
            if k == 3:
                hop("za4", (d,), z_target(d)).wait_recv()
                low = d * (ga // 2)
                read = plus(rows_of(dz, 0, 0), decoder(wire["za4"][1].at[d], ga // 2), low, low + ga // 2)
            else:
                hop("za", (k, d), z_target(d)).wait_recv()
                read = plus(rows_of(dz, 0, 0), decoder(wire["za"][1].at[k, d], ga), 0, ga)
            encode(read, ga, wire["za"][0].at[k - 1, d])
            hop("za", (k - 1, d), z_target(d)).start()

        def b_z(k, n, d):
            dz = k if d == 0 else 8 - k
            dys = (2 - 2 * n, 3 - 2 * n)
            if k == 4:
                reads = [rows_of(4, dy, ra + d * (rb // 2)) for dy in dys]
                encode(joined(reads, gb // 2), gb, wire["zb4"][0].at[n, d])
                hop("zb4", (n, d), z_target(d)).start()
                return
            if k == 3:
                hop("zb4", (n, d), z_target(d)).wait_recv()
                arrived = decoder(wire["zb4"][1].at[n, d], gb)
                low, many = d * (gb // 2), gb // 2
            else:
                hop("zb", (k, n, d), z_target(d)).wait_recv()
                arrived = decoder(wire["zb"][1].at[k, n, d], 2 * gb)
                low, many = 0, gb
            reads = [plus(rows_of(dz, dy, ra), arrived, low, low + many, m * many) for m, dy in enumerate(dys)]
            encode(joined(reads, gb), 2 * gb, wire["zb"][0].at[k - 1, n, d])
            hop("zb", (k - 1, n, d), z_target(d)).start()

        def b_zf(n):
            for d in range(2):
                hop("zb", (0, n, d), z_target(d)).wait_recv()
            left, right = [decoder(wire["zb"][1].at[0, n, d], 2 * gb) for d in range(2)]
            for m in range(2):
                for g in range(gb):
                    part[0, 2 - 2 * n + m, pl.ds(ra + 16 * g, 16), :] += left(m * gb + g) + right(m * gb + g)

        def b_y2(d):
            encode(rows_of(0, 2, ra + d * (rb // 2)), gb // 2, wire["yb2"][0].at[d])
            hop("yb2", (d,), y_target(d)).start()

        def b_y1(d):
            hop("yb2", (d,), y_target(d)).wait_recv()
            low = d * (gb // 2)
            arrived = decoder(wire["yb2"][1].at[d], gb // 2)
            encode(plus(rows_of(0, 1 + 2 * d, ra), arrived, low, low + gb // 2), gb, wire["yb1"][0].at[d])
            hop("yb1", (d,), y_target(d)).start()

        def finish_b():
            for d in range(2):
                hop("yb1", (d,), y_target(d)).wait_recv()
            left, right = [decoder(wire["yb1"][1].at[d], gb) for d in range(2)]
            for g in range(gb):
                store_b(s, g, part[0, 0, pl.ds(ra + 16 * g, 16), :] + left(g) + right(g))

        def finish_a():
            for d in range(2):
                hop("za", (0, d), z_target(d)).wait_recv()
            left, right = [decoder(wire["za"][1].at[0, d], ga) for d in range(2)]
            for g in range(ga):
                grad[0, pl.ds(PROWS * s + 16 * g, 16), :] = part[0, 0, pl.ds(16 * g, 16), :] + left(g) + right(g)

        def drain():
            for d in range(2):
                for k in range(5):
                    hop("ya2", (k, d), y_target(d), len(pairs[k]) * ra // 2 + 16).wait_send()
                    hop("ya1", (k, d), y_target(d), len(pairs[k]) * ra + 16).wait_send()
                hop("za4", (d,), z_target(d)).wait_send()
                hop("yb2", (d,), y_target(d)).wait_send()
                hop("yb1", (d,), y_target(d)).wait_send()
                for k in range(3):
                    hop("za", (k, d), z_target(d)).wait_send()
                    for n in range(2):
                        hop("zb", (k, n, d), z_target(d)).wait_send()
                for n in range(2):
                    hop("zb4", (n, d), z_target(d)).wait_send()

        return {
            "P": produce,
            "AY2": a_y2,
            "AY1": a_y1,
            "AYF": a_yf,
            "AZ": a_z,
            "B": b_z,
            "BF": b_zf,
            "BY2": b_y2,
            "BY1": b_y1,
            "FB": finish_b,
            "FA": finish_a,
            "drain": drain,
        }

    def store_b(s, g, rows):
        if s == 0 or g < 2:
            grad[0, pl.ds(PROWS * s + SLICES[s][0] + 16 * g, 16), :] = rows
        else:
            sec[c, pl.ds(2 * (g - 2), 2)] = rows.reshape(2, 8, BLK)

    def second_rows(h):
        ra = SLICES[1][0]

        @pl.loop(0, SPARE // 2)
        def _(s):
            spill[...] = product_of(table_s[128, 2 * s + c], h).reshape(NQ // 2, 8, BLK)

            @pl.loop(0, NQ // 2)
            def _(r):
                q = r + h * (NQ // 2)
                dz = lax.rem(lax.div(q, NY) - z + NZ, NZ)
                dy = lax.rem(lax.rem(q, NY) - y + NY, NY)
                rings[1]["part"][dz, dy, pl.ds(pl.multiple_of(PROWS + 8 * s, 8), 8), :] = spill[r]

    tasks = [ring(0), ring(1)]
    gather = {
        "gs": gather_start,
        "gf": forward,
        "gsh": share,
        "ge": pass_on,
        "gd": gathered,
        "sec": second_rows,
    }
    for name, s, *rest in ORDER:
        (gather[name] if name in gather else tasks[s][name])(*(([s] if name in gather else []) + rest))
    sec_copy = remote(sec.at[c], sec.at[c], s_sem.at[0], s_sem.at[1], other)
    sec_copy.start()

    sec_copy.wait_recv()

    @pl.loop(0, NQ)
    def _(q):
        place_of = table_s[2 * q + c, 1]
        sec_out[q] = sec[lax.rem(place_of, 2), lax.div(place_of, 2)]

    @pl.loop(1, NQ)
    def _(r):
        q = lax.rem(me_q + r, NQ)
        remote(sec_out.at[q], sec_in.at[me_q], s_sem.at[2], s_sem.at[3], (q * 2 + c, x)).start()

    whole = remote(sec_out.at[pl.ds(0, NQ - 1)], sec_in.at[pl.ds(0, NQ - 1)], s_sem.at[2], s_sem.at[3], other)
    for n in range(4):
        held_in(n).wait()

    def u_whole(k):
        part_of = pl.ds(0, NQ - 1)
        return remote(u_send.at[k, part_of], ret.at[k, c, part_of], u_sem.at[0, k], u_sem.at[1, k], other)

    def u_core(k):
        return remote(ret.at[k, c], ret.at[k, c], r_sem.at[0, k], r_sem.at[1, k], other)

    def finish(k):
        update = refresh(grad[k], held, fresh, k, None if k == 0 else table_s[me_q * 2 + c, 2] > 1)
        for n in range(4):
            fresh_out(n, k).start()
        rows = update.reshape(NQ, 8, BLK)
        halves = jnp.concatenate([rows[:, :, : BLK // 2], rows[:, :, BLK // 2 :]], axis=1)
        u_send[k] = halves.astype(jnp.bfloat16)

        @pl.loop(1, NQ)
        def _(r):
            q = lax.rem(me_q + r, NQ)
            remote(u_send.at[k, q], ret.at[k, c, me_q], u_sem.at[0, k], u_sem.at[1, k], (q * 2 + c, x)).start()

        ret[k, c, me_q] = u_send[k, me_q]

    finish(0)
    whole.wait_recv()
    sec_in[me_q] = sec_out[me_q]
    grad[1] = sec_in[...].reshape(BLK, BLK)
    finish(1)
    for k in range(2):
        u_whole(k).wait_recv()
        u_core(k).start()
    for k in range(2):
        u_core(k).wait_recv()

    ret_copy = pltpu.make_async_copy(ret, ret_out, t_sem)
    ret_copy.start()
    for k in range(2):
        u_whole(k).wait_send()
        u_core(k).wait_send()
        for n in range(4):
            fresh_out(n, k).wait()

    whole.wait_send()
    sec_copy.wait_send()
    cot_copy.wait_send()
    for s in range(2):
        for r in (0, 3, 1):
            core_shard(s, r).wait_send()
        for n in range(4):
            core_piece(s, n).wait_send()
            forward_piece(s, n).wait_send()
        for p in range(3):
            own_piece(s, p, 0).wait_send()
            own_piece(s, p, 1).wait_send()
    tasks[0]["drain"]()
    tasks[1]["drain"]()
    ret_copy.wait()


def hand_over(slots, returned, results):
    def body(slot_ref, ret_hbm, *refs):
        sources, update_ref, targets = refs[:4], refs[4], refs[5:9]
        ret, held, in_sem, out_sem = refs[9:]
        core = lax.rem(lax.axis_index("dp"), 2)
        loads = [pltpu.make_async_copy(sources[n], held.at[n], in_sem.at[n]) for n in range(4)]
        stores = [pltpu.make_async_copy(held.at[n], targets[n], out_sem.at[n]) for n in range(4)]
        rows_in = pltpu.make_async_copy(ret_hbm, ret, in_sem.at[4])
        rows_in.start()
        for load in loads:
            load.start()
        for load, store in zip(loads, stores):
            load.wait()
            store.start()
        rows_in.wait()
        for i in range(12):
            for j in range(6):
                slot = slot_ref[0, 6 * i + j]
                tile = ret[lax.rem(slot, 2), lax.rem(lax.div(slot, 2), 2), lax.div(slot, 4)].astype(jnp.float32)
                for h in range(2):
                    rows = jnp.where(core == 0, tile[8 * h : 8 * h + 4], tile[8 * h + 4 : 8 * h + 8])
                    columns = pl.ds(j * BLK + h * (BLK // 2), BLK // 2)
                    update_ref[i, :, columns] = rows.astype(jnp.bfloat16)
        for store in stores:
            store.wait()

    anywhere = pl.BlockSpec(memory_space=pl.ANY)
    return pl.pallas_call(
        body,
        out_shape=(jax.ShapeDtypeStruct((12, 4, 1536), jnp.bfloat16),)
        + tuple(jax.ShapeDtypeStruct(r.shape, r.dtype) for r in results),
        in_specs=[pl.BlockSpec(memory_space=pltpu.SMEM)] + [anywhere] * 5,
        out_specs=[pl.BlockSpec(memory_space=pltpu.VMEM)] + [anywhere] * 4,
        scratch_shapes=[
            pltpu.VMEM(returned.shape, returned.dtype),
            pltpu.VMEM((4, 2, BLK, BLK), jnp.float32),
            pltpu.SemaphoreType.DMA((5,)),
            pltpu.SemaphoreType.DMA((4,)),
        ],
    )(slots, returned, *results)


def on_device(
    activations, cotangent, block_owner, left_factor, right_factor, left_basis, right_basis
):
    token_scale = 1.0 / math.sqrt(activations.shape[0] * lax.axis_size("dp"))
    i16, f32, i32, bf16 = jnp.int16, jnp.float32, jnp.int32, jnp.bfloat16
    vmem, dma = pltpu.VMEM, pltpu.SemaphoreType.DMA

    def pair(*shape):
        return (vmem(shape + (BLK,), i16), vmem(shape + (BLK,), i16))

    def ring_scratch(ra, rb):
        return dict(
            part=vmem((NZ, NY, ra + rb, BLK), f32),
            wire=dict(
                ya2=pair(5, 2, ra + 16),
                ya1=pair(5, 2, 2 * ra + 16),
                za4=pair(2, ra // 2 + 16),
                za=pair(3, 2, ra + 16),
                zb4=pair(2, 2, rb + 16),
                zb=pair(3, 2, 2, 2 * rb + 16),
                yb2=pair(2, rb // 2 + 16),
                yb1=pair(2, rb + 16),
            ),
            sems=dict(
                ya2=dma((2, 5, 2)),
                ya1=dma((2, 5, 2)),
                za4=dma((2, 2)),
                za=dma((2, 3, 2)),
                zb4=dma((2, 2, 2)),
                zb=dma((2, 3, 2, 2)),
                yb2=dma((2, 2)),
                yb1=dma((2, 2)),
            ),
        )

    whole = pl.BlockSpec(memory_space=pltpu.VMEM)
    anywhere = pl.BlockSpec(memory_space=pl.ANY)
    slots, returned, *results = pl.pallas_call(
        functools.partial(gradient_kernel, token_scale),
        out_shape=(jax.ShapeDtypeStruct((1, 72), i32), jax.ShapeDtypeStruct((2, 2, NQ, 16, BLK // 2), bf16))
        + tuple(jax.ShapeDtypeStruct((2, BLK, BLK), f32) for _ in range(4)),
        in_specs=[whole] + [anywhere] * 6,
        out_specs=[whole] + [anywhere] * 5,
        scratch_shapes=[
            vmem((1, 128), i32),
            vmem((512, 768), bf16),
            vmem((4, 2, BLK, BLK), f32),
            vmem((4, 2, BLK, BLK), f32),
            vmem((2, BLK, BLK), f32),
            vmem((2, NQ, 16, BLK // 2), bf16),
            vmem((2, 2, NQ, 16, BLK // 2), bf16),
            vmem((136, 128), i32),
            pltpu.SMEM((136, 128), i32),
            tuple(vmem((2, 3 * NX, PROWS, 512), bf16) for _ in SLICES),
            vmem((2, 6, 512, BLK), bf16),
            vmem((NQ // 2, 8, BLK), f32),
            tuple(ring_scratch(*rows) for rows in SLICES),
            vmem((2, SPARE // 2, 8, BLK), f32),
            vmem((NQ, 8, BLK), f32),
            vmem((NQ, 8, BLK), f32),
            dma((2, 2, 3)),
            dma((2, 2, 3)),
            dma((2, 4)),
            dma((2, 4)),
            dma((2, 8)),
            dma((2, 8)),
            dma,
            dma((4,)),
            dma((8,)),
            dma((4,)),
            dma((4, 2)),
            dma((2, 2)),
            dma((2, 2)),
        ],
        compiler_params=pltpu.CompilerParams(
            collective_id=0, has_side_effects=True, vmem_limit_bytes=58 * 1024 * 1024
        ),
    )(block_owner.reshape(1, 72), activations, cotangent, left_factor, right_factor, left_basis, right_basis)
    update, *results = hand_over(slots, returned, results)
    return (jnp.swapaxes(update, 0, 1), *results)


def solution(mesh):
    placed = (
        P("dp", "mp"),
        P("dp", "mp"),
        P(),
        P("dp", "mp", None),
        P("dp", "mp", None),
        P("dp", "mp", None),
        P("dp", "mp", None),
    )
    return jax.shard_map(
        on_device,
        mesh=mesh,
        in_specs=placed,
        out_specs=(
            P("dp", None, "mp"),
            P("dp", "mp", None),
            P("dp", "mp", None),
            P("dp", "mp", None),
            P("dp", "mp", None),
        ),
        check_vma=False,
    )
```

```python
import functools
import math

import jax
import jax.numpy as jnp
from jax import lax
from jax.experimental import pallas as pl
from jax.experimental.pallas import tpu as pltpu
from jax.sharding import PartitionSpec as P

NSTEPS = 6
BETA = 0.9
EPS = 1e-06
MESH = pl.DeviceIdType.MESH
NX, NY, NZ, NQ = 4, 4, 8, 32
BLK = 256
SLICES = ((64, 64), (96, 64))
SPARE = 8
PROWS = 128
ORDER = (
    ("gf", 0, 1),
    ("gf", 0, 0),
    ("gf", 0, 3),
    ("gf", 0, 2),
    ("gs", 1),
    ("gsh", 0),
    ("ge", 0, 1),
    ("ge", 0, 0),
    ("ge", 0, 2),
    ("ge", 0, 3),
    ("gd", 0),
    ("P", 0, 4),
    ("AY2", 0, 4, 0),
    ("B", 0, 4, 0, 0),
    ("B", 0, 4, 0, 1),
    ("AY2", 0, 4, 1),
    ("gf", 1, 1),
    ("B", 0, 4, 1, 0),
    ("B", 0, 4, 1, 1),
    ("P", 0, 2),
    ("P", 0, 5),
    ("gf", 1, 0),
    ("P", 0, 3),
    ("AY2", 0, 3, 0),
    ("gf", 1, 2),
    ("B", 0, 3, 0, 0),
    ("B", 0, 3, 0, 1),
    ("AY1", 0, 4, 1),
    ("sec", 0),
    ("gf", 1, 3),
    ("AY2", 0, 3, 1),
    ("AY1", 0, 4, 0),
    ("B", 0, 3, 1, 0),
    ("gsh", 1),
    ("P", 0, 1),
    ("AY1", 0, 3, 0),
    ("B", 0, 3, 1, 1),
    ("P", 0, 6),
    ("ge", 1, 1),
    ("ge", 1, 0),
    ("P", 0, 7),
    ("AY2", 0, 2, 1),
    ("ge", 1, 2),
    ("AYF", 0, 4),
    ("AZ", 0, 4, 1),
    ("ge", 1, 3),
    ("B", 0, 2, 1, 0),
    ("AY2", 0, 2, 0),
    ("B", 0, 2, 0, 0),
    ("AY2", 0, 1, 0),
    ("B", 0, 2, 0, 1),
    ("AY1", 0, 3, 1),
    ("gd", 1),
    ("P", 1, 4),
    ("AY2", 1, 4, 0),
    ("sec", 1),
    ("AZ", 0, 4, 0),
    ("B", 1, 4, 0, 1),
    ("B", 1, 4, 1, 1),
    ("B", 1, 4, 0, 0),
    ("P", 1, 3),
    ("B", 1, 4, 1, 0),
    ("AY2", 1, 4, 1),
    ("P", 1, 5),
    ("AY2", 1, 3, 1),
    ("P", 1, 2),
    ("B", 1, 3, 0, 1),
    ("AY1", 1, 4, 0),
    ("AY2", 0, 1, 1),
    ("B", 1, 3, 0, 0),
    ("B", 1, 3, 1, 1),
    ("AY2", 1, 3, 0),
    ("AY1", 1, 4, 1),
    ("AY1", 0, 2, 0),
    ("P", 1, 6),
    ("AY2", 1, 2, 1),
    ("AYF", 0, 3),
    ("B", 1, 3, 1, 0),
    ("B", 0, 2, 1, 1),
    ("AY1", 1, 3, 1),
    ("AY2", 1, 2, 0),
    ("AZ", 0, 3, 1),
    ("AZ", 0, 3, 0),
    ("P", 1, 1),
    ("B", 1, 2, 0, 0),
    ("AYF", 1, 4),
    ("B", 1, 2, 0, 1),
    ("AY1", 1, 3, 0),
    ("AZ", 1, 4, 0),
    ("AY1", 0, 2, 1),
    ("AY1", 0, 1, 1),
    ("B", 1, 2, 1, 1),
    ("P", 1, 7),
    ("AY2", 1, 1, 0),
    ("B", 0, 1, 1, 0),
    ("P", 1, 0),
    ("AZ", 1, 4, 1),
    ("AY2", 1, 0, 0),
    ("AY2", 1, 0, 1),
    ("B", 1, 2, 1, 0),
    ("B", 0, 1, 0, 1),
    ("AY1", 1, 2, 0),
    ("AY2", 1, 1, 1),
    ("AY1", 1, 2, 1),
    ("AY1", 0, 1, 0),
    ("B", 1, 1, 0, 0),
    ("AYF", 0, 2),
    ("AYF", 1, 3),
    ("B", 1, 1, 0, 1),
    ("P", 0, 0),
    ("B", 0, 1, 0, 0),
    ("AZ", 1, 3, 1),
    ("B", 1, 1, 1, 1),
    ("AY2", 0, 0, 1),
    ("AZ", 1, 3, 0),
    ("AY2", 0, 0, 0),
    ("AY1", 1, 1, 0),
    ("B", 1, 1, 1, 0),
    ("AY1", 1, 1, 1),
    ("AZ", 0, 2, 0),
    ("BF", 1, 0),
    ("B", 0, 1, 1, 1),
    ("AZ", 0, 2, 1),
    ("BY2", 1, 0),
    ("BY2", 1, 1),
    ("BF", 0, 0),
    ("BY2", 0, 1),
    ("BY2", 0, 0),
    ("AY1", 0, 0, 0),
    ("AY1", 0, 0, 1),
    ("AYF", 1, 2),
    ("AZ", 1, 2, 0),
    ("AZ", 1, 2, 1),
    ("AY1", 1, 0, 1),
    ("AY1", 1, 0, 0),
    ("AYF", 1, 1),
    ("BY1", 1, 1),
    ("BF", 1, 1),
    ("BY1", 1, 0),
    ("BF", 0, 1),
    ("AYF", 0, 1),
    ("BY1", 0, 1),
    ("AZ", 0, 1, 0),
    ("BY1", 0, 0),
    ("AZ", 0, 1, 1),
    ("AZ", 1, 1, 1),
    ("AZ", 1, 1, 0),
    ("FB", 1),
    ("sx", 1),
    ("AYF", 0, 0),
    ("AYF", 1, 0),
    ("FA", 0),
    ("FB", 0),
    ("sw", 1),
    ("FA", 1),
)


def place():
    dp = lax.axis_index("dp")
    x = lax.axis_index("mp")
    return x, lax.rem(lax.div(dp, 2), NY), lax.div(dp, 2 * NY), lax.rem(dp, 2)


def device(dx=0, dy=0, dz=0, dc=0):
    x, y, z, c = place()
    x = lax.rem(x + dx + NX, NX)
    y = lax.rem(y + dy + NY, NY)
    z = lax.rem(z + dz + NZ, NZ)
    c = lax.rem(c + dc, 2)
    return ((z * NY + y) * 2 + c, x)


def remote(src, dst, send, recv, target):
    return pltpu.make_async_remote_copy(
        src_ref=src, dst_ref=dst, send_sem=send, recv_sem=recv, device_id=target, device_id_type=MESH
    )


def encode(read, groups, dst):
    exponents = []
    for g in range(groups):
        value = read(g)
        top = jnp.max(jnp.abs(value), axis=0, keepdims=True)
        exponent = jnp.ceil(jnp.log2(jnp.maximum(top, 1e-30) * (1.0 / 32700.0)))
        exponents.append(exponent)
        coded = jnp.round(value * jnp.exp2(-exponent))
        dst[pl.ds(16 * g, 16), :] = coded.astype(jnp.int32).astype(jnp.int16)
    exponents.append(jnp.zeros((16 - groups, BLK), jnp.float32))
    tile = jnp.concatenate(exponents, axis=0)
    dst[pl.ds(16 * groups, 16), :] = tile.astype(jnp.int32).astype(jnp.int16)


def decoder(src, groups):
    scales = jnp.exp2(src[pl.ds(16 * groups, 16), :].astype(jnp.int32).astype(jnp.float32))

    def read(g):
        value = src[pl.ds(16 * g, 16), :].astype(jnp.int32).astype(jnp.float32)
        return value * scales[g : g + 1, :]

    return read


def split(value):
    high = value.astype(jnp.bfloat16)
    return high, (value - high.astype(jnp.float32)).astype(jnp.bfloat16)


def turned(parts):
    return parts[0].T, parts[1].T


def times(left_parts, right_parts):
    def dot(a, b):
        return jnp.dot(a, b, preferred_element_type=jnp.float32)

    both = dot(jnp.concatenate(left_parts, axis=0), right_parts[0])
    return both[:BLK] + (both[BLK:] + dot(left_parts[0], right_parts[1]))


def refresh(gradient, held, fresh, k, live):
    def keep(n, value):
        fresh[n, k] = value if live is None else jnp.where(live, value, held[n, k])

    g = split(gradient)
    gt = turned(g)
    share = (1.0 - BETA) / BLK
    factors = [BETA * held[0, k] + share * times(g, gt), BETA * held[1, k] + share * times(gt, g)]
    powers, scales = [], []
    for n in range(2):
        keep(n, factors[n])
        power = times(split(factors[n]), split(held[2 + n, k]))
        square = jnp.sum(power * power, axis=0, keepdims=True)
        scales.append(jnp.exp(-0.125 * jnp.log(square * (1.0 / BLK) + EPS)))
        powers.append(power / jnp.sqrt(jnp.sum(square, axis=1, keepdims=True) + EPS))

    def step(_, values):
        parts = [split(v) for v in values]
        grams = [times(turned(p), p) for p in parts]
        moves = [times(p, split(gram)) for p, gram in zip(parts, grams)]
        return tuple(1.5 * v - 0.5 * m for v, m in zip(values, moves))

    bases = lax.fori_loop(0, NSTEPS, step, tuple(powers))
    weights = []
    for n in range(2):
        keep(2 + n, bases[n])
        weights.append(times(split(bases[n] * scales[n]), turned(split(bases[n]))))
    inner = times(g, split(weights[1]))
    return times(split(weights[0]), split(inner))


def gradient_kernel(
    token_scale,
    owner_ref,
    act_hbm,
    cot_hbm,
    left_hbm,
    right_hbm,
    left_basis_hbm,
    right_basis_hbm,
    slots_out,
    ret_out,
    left_out,
    right_out,
    left_basis_out,
    right_basis_out,
    owner_v,
    act_ref,
    held,
    fresh,
    grad,
    u_send,
    ret,
    table_v,
    table_s,
    at,
    cot2,
    spill,
    rings,
    sec,
    sec_out,
    sec_in,
    x_send,
    x_recv,
    f_send,
    f_recv,
    c_send,
    c_recv,
    t_sem,
    s_sem,
    in_sem,
    held_sem,
    out_sem,
    u_sem,
    r_sem,
):
    x, y, z, c = place()
    me_q = z * NY + y
    other = device(dc=1)

    def act_in(n):
        columns = pl.ds(n * 384, 384)
        return pltpu.make_async_copy(act_hbm.at[:, columns], act_ref.at[:, columns], in_sem.at[6 + n])

    def cot_in(j):
        return pltpu.make_async_copy(cot_hbm.at[:, pl.ds(j * BLK, BLK)], cot2.at[0, j], in_sem.at[j])

    factors = (left_hbm, right_hbm, left_basis_hbm, right_basis_hbm)
    results = (left_out, right_out, left_basis_out, right_basis_out)

    def held_in(n):
        return pltpu.make_async_copy(factors[n], held.at[n], held_sem.at[n])

    def fresh_out(n, k):
        return pltpu.make_async_copy(fresh.at[n, k], results[n].at[k], out_sem.at[n, k])

    barrier = pltpu.get_barrier_semaphore()
    act_in(0).start()
    act_in(1).start()
    neighbours = [device(dx=1), device(dx=3), device(dy=1), device(dy=3), device(dz=1), device(dz=7), other]
    for target in neighbours:
        pl.semaphore_signal(barrier, inc=1, device_id=target, device_id_type=MESH)
    for j in range(6):
        cot_in(j).start()

    def turn(s, p):
        at[s][0, p] = act_ref[:, pl.ds(p * BLK + s * PROWS, PROWS)].T

    def own_piece(s, p, d):
        sgn = 1 - 2 * d
        return remote(
            at[s].at[0, p],
            at[s].at[0, 3 * ((4 - sgn) % 4) + p],
            x_send.at[s, d, p],
            x_recv.at[s, d, p],
            device(dx=sgn),
        )

    far = ((0, 0, 128, 0), (2, 0, 128, 1), (1, 0, 64, 0), (1, 64, 64, 1))

    def forward_piece(s, n):
        p, start, size, d = far[n]
        sgn = 1 - 2 * d
        rows = pl.ds(start, size)
        return remote(
            at[s].at[0, 3 * ((4 - sgn) % 4) + p, rows],
            at[s].at[0, 6 + p, rows],
            f_send.at[s, n],
            f_recv.at[s, n],
            device(dx=sgn),
        )

    def core_shard(s, r):
        rows = pl.ds(3 * r, 3)
        n = {0: 0, 3: 1, 1: 2}[r]
        return remote(at[s].at[0, rows], at[s].at[1, rows], c_send.at[s, n], c_recv.at[s, n], other)

    def core_piece(s, n):
        p, start, size, _ = far[n]
        rows = pl.ds(start, size)
        return remote(
            at[s].at[0, 6 + p, rows], at[s].at[1, 6 + p, rows], c_send.at[s, 3 + n], c_recv.at[s, 3 + n], other
        )

    def gather_start(s):
        for n in range(3):
            own_piece(s, n, 0).start()
            own_piece(s, 2 - n, 1).start()
        core_shard(s, 0).start()

    def forward(s, n):
        p, _, _, d = far[n]
        own_piece(s, p, d).wait_recv()
        forward_piece(s, n).start()

    def share(s):
        own_piece(s, 2, 0).wait_recv()
        own_piece(s, 0, 1).wait_recv()
        core_shard(s, 3).start()
        core_shard(s, 1).start()

    def pass_on(s, n):
        forward_piece(s, n).wait_recv()
        core_piece(s, n).start()

    def gathered(s):
        for r in (0, 3, 1):
            core_shard(s, r).wait_recv()
        for n in range(4):
            core_piece(s, n).wait_recv()
        if s == 0:
            cot_copy.wait_recv()

    act_in(0).wait()
    act_in(1).wait()
    for p in (0, 2, 1):
        turn(0, p)
    pl.semaphore_wait(barrier, 7)
    gather_start(0)
    for n in range(4):
        held_in(n).start()
    for j in range(6):
        cot_in(j).wait()
    cot_copy = remote(cot2.at[0], cot2.at[1], c_send.at[0, 7], c_recv.at[0, 7], other)
    cot_copy.start()
    for p in range(3):
        turn(1, p)

    owner_v[...] = jnp.full((1, 128), -1, jnp.int32)
    owner_v[:, pl.ds(0, 72)] = owner_ref[...]
    owners = owner_v[...]
    lanes = lax.broadcasted_iota(jnp.int32, (128, 128), 1)
    subs = lax.broadcasted_iota(jnp.int32, (128, 128), 0)
    earlier = lanes < subs
    owner_column = jnp.broadcast_to(owners, (128, 128)).T
    same = owner_column == owners
    is_second = jnp.max(jnp.where(same & earlier & (subs < 72), 1, 0), axis=1, keepdims=True)
    is_second = jnp.broadcast_to(is_second, (128, 128))
    second_row = is_second.T
    rank = jnp.sum(jnp.where(earlier, second_row, 0), axis=1, keepdims=True)
    rank = jnp.broadcast_to(rank, (128, 128))
    rank_row = rank.T
    mine = owners == subs
    first = jnp.min(jnp.where(mine, lanes, 71), axis=1, keepdims=True)
    entry = jnp.sum(jnp.where(mine, second_row * rank_row, 0), axis=1, keepdims=True)
    numbers = jnp.sum(jnp.where(rank == lanes, is_second * subs, 0), axis=0, keepdims=True)
    entry = jnp.minimum(entry, SPARE - 1)
    count = jnp.sum(jnp.where(mine, 1, 0), axis=1, keepdims=True)
    columns = jnp.where(lanes == 0, first, jnp.where(lanes == 1, entry, count))
    table_v[0:128, :] = columns
    table_v[128:136, :] = jnp.broadcast_to(numbers, (8, 128))
    slots_out[...] = (2 * owners + second_row[0:1, :])[:, 0:72]
    table_copy = pltpu.make_async_copy(table_v, table_s, t_sem)
    table_copy.start()
    table_copy.wait()

    def product_of(block, s):
        band = lax.rem(lax.div(block, 6) - 3 * x + 12, 12)
        column = lax.rem(block, 6)
        total = jnp.dot(at[s][0, band], cot2[0, column], preferred_element_type=jnp.float32)
        total += jnp.dot(at[s][1, band], cot2[1, column], preferred_element_type=jnp.float32)
        return total * token_scale

    def ring(s):
        ra, rb = SLICES[s]
        part = rings[s]["part"]
        wire = rings[s]["wire"]
        sems = rings[s]["sems"]

        def hop(name, index, target, rows=None):
            src, dst = wire[name]
            send, recv = sems[name].at[(0,) + index], sems[name].at[(1,) + index]
            if rows is not None:
                index = index + (pl.ds(0, rows),)
            return remote(src.at[index], dst.at[index], send, recv, target)

        def produce(dz):
            @pl.loop(0, NY)
            def _(dy):
                q = lax.rem(z + dz, NZ) * NY + lax.rem(y + dy, NY)
                part[dz, dy, pl.ds(0, PROWS), :] = product_of(table_s[2 * q + c, 0], s)

        def rows_of(dz, dy, start):
            def read(g):
                return part[dz, dy, pl.ds(start + 16 * g, 16), :]

            return read

        def joined(reads, groups):
            def read(g):
                return reads[g // groups](g % groups)

            return read

        def plus(first_read, second_read, low, high, shift=0):
            def read(g):
                if low <= g < high:
                    return first_read(g) + second_read(g - low + shift)
                return first_read(g)

            return read

        ga, gb = ra // 16, rb // 16
        pairs = {4: (4,), 3: (3, 5), 2: (2, 6), 1: (1, 7), 0: (0,)}

        def y_target(d):
            return device(dy=1 - 2 * d)

        def z_target(d):
            return device(dz=1 - 2 * d)

        def a_y2(k, d):
            rows = len(pairs[k]) * ra // 2 + 16
            reads = [rows_of(dz, 2, d * (ra // 2)) for dz in pairs[k]]
            encode(joined(reads, ga // 2), len(reads) * ga // 2, wire["ya2"][0].at[k, d])
            hop("ya2", (k, d), y_target(d), rows).start()

        def a_y1(k, d):
            count = len(pairs[k])
            hop("ya2", (k, d), y_target(d), count * ra // 2 + 16).wait_recv()
            arrived = decoder(wire["ya2"][1].at[k, d], count * ga // 2)
            low = d * (ga // 2)
            reads = [
                plus(rows_of(dz, 1 + 2 * d, 0), arrived, low, low + ga // 2, n * (ga // 2))
                for n, dz in enumerate(pairs[k])
            ]
            encode(joined(reads, ga), count * ga, wire["ya1"][0].at[k, d])
            hop("ya1", (k, d), y_target(d), count * ra + 16).start()

        def a_yf(k):
            count = len(pairs[k])
            for d in range(2):
                hop("ya1", (k, d), y_target(d), count * ra + 16).wait_recv()
            left, right = [decoder(wire["ya1"][1].at[k, d], count * ga) for d in range(2)]
            for n, dz in enumerate(pairs[k]):
                for g in range(ga):
                    part[dz, 0, pl.ds(16 * g, 16), :] += left(n * ga + g) + right(n * ga + g)

        def a_z(k, d):
            dz = k if d == 0 else 8 - k
            if k == 4:
                encode(rows_of(4, 0, d * (ra // 2)), ga // 2, wire["za4"][0].at[d])
                hop("za4", (d,), z_target(d)).start()
                return
            if k == 3:
                hop("za4", (d,), z_target(d)).wait_recv()
                low = d * (ga // 2)
                read = plus(rows_of(dz, 0, 0), decoder(wire["za4"][1].at[d], ga // 2), low, low + ga // 2)
            else:
                hop("za", (k, d), z_target(d)).wait_recv()
                read = plus(rows_of(dz, 0, 0), decoder(wire["za"][1].at[k, d], ga), 0, ga)
            encode(read, ga, wire["za"][0].at[k - 1, d])
            hop("za", (k - 1, d), z_target(d)).start()

        def b_z(k, n, d):
            dz = k if d == 0 else 8 - k
            dys = (2 - 2 * n, 3 - 2 * n)
            if k == 4:
                reads = [rows_of(4, dy, ra + d * (rb // 2)) for dy in dys]
                encode(joined(reads, gb // 2), gb, wire["zb4"][0].at[n, d])
                hop("zb4", (n, d), z_target(d)).start()
                return
            if k == 3:
                hop("zb4", (n, d), z_target(d)).wait_recv()
                arrived = decoder(wire["zb4"][1].at[n, d], gb)
                low, many = d * (gb // 2), gb // 2
            else:
                hop("zb", (k, n, d), z_target(d)).wait_recv()
                arrived = decoder(wire["zb"][1].at[k, n, d], 2 * gb)
                low, many = 0, gb
            reads = [plus(rows_of(dz, dy, ra), arrived, low, low + many, m * many) for m, dy in enumerate(dys)]
            encode(joined(reads, gb), 2 * gb, wire["zb"][0].at[k - 1, n, d])
            hop("zb", (k - 1, n, d), z_target(d)).start()

        def b_zf(n):
            for d in range(2):
                hop("zb", (0, n, d), z_target(d)).wait_recv()
            left, right = [decoder(wire["zb"][1].at[0, n, d], 2 * gb) for d in range(2)]
            for m in range(2):
                for g in range(gb):
                    part[0, 2 - 2 * n + m, pl.ds(ra + 16 * g, 16), :] += left(m * gb + g) + right(m * gb + g)

        def b_y2(d):
            encode(rows_of(0, 2, ra + d * (rb // 2)), gb // 2, wire["yb2"][0].at[d])
            hop("yb2", (d,), y_target(d)).start()

        def b_y1(d):
            hop("yb2", (d,), y_target(d)).wait_recv()
            low = d * (gb // 2)
            arrived = decoder(wire["yb2"][1].at[d], gb // 2)
            encode(plus(rows_of(0, 1 + 2 * d, ra), arrived, low, low + gb // 2), gb, wire["yb1"][0].at[d])
            hop("yb1", (d,), y_target(d)).start()

        def finish_b():
            for d in range(2):
                hop("yb1", (d,), y_target(d)).wait_recv()
            left, right = [decoder(wire["yb1"][1].at[d], gb) for d in range(2)]
            for g in range(gb):
                store_b(s, g, part[0, 0, pl.ds(ra + 16 * g, 16), :] + left(g) + right(g))

        def finish_a():
            for d in range(2):
                hop("za", (0, d), z_target(d)).wait_recv()
            left, right = [decoder(wire["za"][1].at[0, d], ga) for d in range(2)]
            for g in range(ga):
                grad[0, pl.ds(PROWS * s + 16 * g, 16), :] = part[0, 0, pl.ds(16 * g, 16), :] + left(g) + right(g)

        def drain():
            for d in range(2):
                for k in range(5):
                    hop("ya2", (k, d), y_target(d), len(pairs[k]) * ra // 2 + 16).wait_send()
                    hop("ya1", (k, d), y_target(d), len(pairs[k]) * ra + 16).wait_send()
                hop("za4", (d,), z_target(d)).wait_send()
                hop("yb2", (d,), y_target(d)).wait_send()
                hop("yb1", (d,), y_target(d)).wait_send()
                for k in range(3):
                    hop("za", (k, d), z_target(d)).wait_send()
                    for n in range(2):
                        hop("zb", (k, n, d), z_target(d)).wait_send()
                for n in range(2):
                    hop("zb4", (n, d), z_target(d)).wait_send()

        return {
            "P": produce,
            "AY2": a_y2,
            "AY1": a_y1,
            "AYF": a_yf,
            "AZ": a_z,
            "B": b_z,
            "BF": b_zf,
            "BY2": b_y2,
            "BY1": b_y1,
            "FB": finish_b,
            "FA": finish_a,
            "drain": drain,
        }

    def store_b(s, g, rows):
        if s == 0 or g < 2:
            grad[0, pl.ds(PROWS * s + SLICES[s][0] + 16 * g, 16), :] = rows
        else:
            sec[c, pl.ds(2 * (g - 2), 2)] = rows.reshape(2, 8, BLK)

    def second_rows(h):
        ra = SLICES[1][0]

        @pl.loop(0, SPARE // 2)
        def _(s):
            spill[...] = product_of(table_s[128, 2 * s + c], h).reshape(NQ // 2, 8, BLK)

            @pl.loop(0, NQ // 2)
            def _(r):
                q = r + h * (NQ // 2)
                dz = lax.rem(lax.div(q, NY) - z + NZ, NZ)
                dy = lax.rem(lax.rem(q, NY) - y + NY, NY)
                rings[1]["part"][dz, dy, pl.ds(pl.multiple_of(PROWS + 8 * s, 8), 8), :] = spill[r]

    sec_copy = remote(sec.at[c], sec.at[c], s_sem.at[0], s_sem.at[1], other)

    def second_share(_):
        sec_copy.start()

    def second_send(_):
        sec_copy.wait_recv()

        @pl.loop(0, NQ, unroll=True)
        def _(q):
            place_of = table_s[2 * q + c, 1]
            sec_out[q] = sec[lax.rem(place_of, 2), lax.div(place_of, 2)]

        @pl.loop(1, NQ, unroll=True)
        def _(r):
            q = lax.rem(me_q + r, NQ)
            remote(sec_out.at[q], sec_in.at[me_q], s_sem.at[2], s_sem.at[3], (q * 2 + c, x)).start()

    tasks = [ring(0), ring(1)]
    gather = {
        "gs": gather_start,
        "gf": forward,
        "gsh": share,
        "ge": pass_on,
        "gd": gathered,
        "sec": second_rows,
        "sx": second_share,
        "sw": second_send,
    }
    for name, s, *rest in ORDER:
        (gather[name] if name in gather else tasks[s][name])(*(([s] if name in gather else []) + rest))
    whole = remote(sec_out.at[pl.ds(0, NQ - 1)], sec_in.at[pl.ds(0, NQ - 1)], s_sem.at[2], s_sem.at[3], other)
    for n in range(4):
        held_in(n).wait()

    def u_whole(k):
        part_of = pl.ds(0, NQ - 1)
        return remote(u_send.at[k, part_of], ret.at[k, c, part_of], u_sem.at[0, k], u_sem.at[1, k], other)

    def u_core(k):
        return remote(ret.at[k, c], ret.at[k, c], r_sem.at[0, k], r_sem.at[1, k], other)

    def finish(k):
        update = refresh(grad[k], held, fresh, k, None if k == 0 else table_s[me_q * 2 + c, 2] > 1)
        for n in range(4):
            fresh_out(n, k).start()
        rows = update.reshape(NQ, 8, BLK)
        halves = jnp.concatenate([rows[:, :, : BLK // 2], rows[:, :, BLK // 2 :]], axis=1)
        u_send[k] = halves.astype(jnp.bfloat16)

        @pl.loop(1, NQ, unroll=True)
        def _(r):
            q = lax.rem(me_q + r, NQ)
            remote(u_send.at[k, q], ret.at[k, c, me_q], u_sem.at[0, k], u_sem.at[1, k], (q * 2 + c, x)).start()

        ret[k, c, me_q] = u_send[k, me_q]

    finish(0)
    whole.wait_recv()
    sec_in[me_q] = sec_out[me_q]
    grad[1] = sec_in[...].reshape(BLK, BLK)
    finish(1)
    for k in range(2):
        u_whole(k).wait_recv()
        u_core(k).start()
    for k in range(2):
        u_core(k).wait_recv()

    ret_copy = pltpu.make_async_copy(ret, ret_out, t_sem)
    ret_copy.start()
    for k in range(2):
        u_whole(k).wait_send()
        u_core(k).wait_send()
        for n in range(4):
            fresh_out(n, k).wait()

    whole.wait_send()
    sec_copy.wait_send()
    cot_copy.wait_send()
    for s in range(2):
        for r in (0, 3, 1):
            core_shard(s, r).wait_send()
        for n in range(4):
            core_piece(s, n).wait_send()
            forward_piece(s, n).wait_send()
        for p in range(3):
            own_piece(s, p, 0).wait_send()
            own_piece(s, p, 1).wait_send()
    tasks[0]["drain"]()
    tasks[1]["drain"]()
    ret_copy.wait()


def hand_over(slots, returned, results):
    def body(slot_ref, ret_hbm, *refs):
        sources, update_ref, targets = refs[:4], refs[4], refs[5:9]
        ret, held, in_sem, out_sem = refs[9:]
        core = lax.rem(lax.axis_index("dp"), 2)
        loads = [pltpu.make_async_copy(sources[n], held.at[n], in_sem.at[n]) for n in range(4)]
        stores = [pltpu.make_async_copy(held.at[n], targets[n], out_sem.at[n]) for n in range(4)]
        rows_in = pltpu.make_async_copy(ret_hbm, ret, in_sem.at[4])
        rows_in.start()
        for load in loads:
            load.start()
        for load, store in zip(loads, stores):
            load.wait()
            store.start()
        rows_in.wait()
        for i in range(12):
            for j in range(6):
                slot = slot_ref[0, 6 * i + j]
                tile = ret[lax.rem(slot, 2), lax.rem(lax.div(slot, 2), 2), lax.div(slot, 4)].astype(jnp.float32)
                for h in range(2):
                    rows = jnp.where(core == 0, tile[8 * h : 8 * h + 4], tile[8 * h + 4 : 8 * h + 8])
                    columns = pl.ds(j * BLK + h * (BLK // 2), BLK // 2)
                    update_ref[i, :, columns] = rows.astype(jnp.bfloat16)
        for store in stores:
            store.wait()

    anywhere = pl.BlockSpec(memory_space=pl.ANY)
    return pl.pallas_call(
        body,
        out_shape=(jax.ShapeDtypeStruct((12, 4, 1536), jnp.bfloat16),)
        + tuple(jax.ShapeDtypeStruct(r.shape, r.dtype) for r in results),
        in_specs=[pl.BlockSpec(memory_space=pltpu.SMEM)] + [anywhere] * 5,
        out_specs=[pl.BlockSpec(memory_space=pltpu.VMEM)] + [anywhere] * 4,
        scratch_shapes=[
            pltpu.VMEM(returned.shape, returned.dtype),
            pltpu.VMEM((4, 2, BLK, BLK), jnp.float32),
            pltpu.SemaphoreType.DMA((5,)),
            pltpu.SemaphoreType.DMA((4,)),
        ],
    )(slots, returned, *results)


def on_device(
    activations, cotangent, block_owner, left_factor, right_factor, left_basis, right_basis
):
    token_scale = 1.0 / math.sqrt(activations.shape[0] * lax.axis_size("dp"))
    i16, f32, i32, bf16 = jnp.int16, jnp.float32, jnp.int32, jnp.bfloat16
    vmem, dma = pltpu.VMEM, pltpu.SemaphoreType.DMA

    def pair(*shape):
        return (vmem(shape + (BLK,), i16), vmem(shape + (BLK,), i16))

    def ring_scratch(ra, rb):
        return dict(
            part=vmem((NZ, NY, ra + rb, BLK), f32),
            wire=dict(
                ya2=pair(5, 2, ra + 16),
                ya1=pair(5, 2, 2 * ra + 16),
                za4=pair(2, ra // 2 + 16),
                za=pair(3, 2, ra + 16),
                zb4=pair(2, 2, rb + 16),
                zb=pair(3, 2, 2, 2 * rb + 16),
                yb2=pair(2, rb // 2 + 16),
                yb1=pair(2, rb + 16),
            ),
            sems=dict(
                ya2=dma((2, 5, 2)),
                ya1=dma((2, 5, 2)),
                za4=dma((2, 2)),
                za=dma((2, 3, 2)),
                zb4=dma((2, 2, 2)),
                zb=dma((2, 3, 2, 2)),
                yb2=dma((2, 2)),
                yb1=dma((2, 2)),
            ),
        )

    whole = pl.BlockSpec(memory_space=pltpu.VMEM)
    anywhere = pl.BlockSpec(memory_space=pl.ANY)
    slots, returned, *results = pl.pallas_call(
        functools.partial(gradient_kernel, token_scale),
        out_shape=(jax.ShapeDtypeStruct((1, 72), i32), jax.ShapeDtypeStruct((2, 2, NQ, 16, BLK // 2), bf16))
        + tuple(jax.ShapeDtypeStruct((2, BLK, BLK), f32) for _ in range(4)),
        in_specs=[whole] + [anywhere] * 6,
        out_specs=[whole] + [anywhere] * 5,
        scratch_shapes=[
            vmem((1, 128), i32),
            vmem((512, 768), bf16),
            vmem((4, 2, BLK, BLK), f32),
            vmem((4, 2, BLK, BLK), f32),
            vmem((2, BLK, BLK), f32),
            vmem((2, NQ, 16, BLK // 2), bf16),
            vmem((2, 2, NQ, 16, BLK // 2), bf16),
            vmem((136, 128), i32),
            pltpu.SMEM((136, 128), i32),
            tuple(vmem((2, 3 * NX, PROWS, 512), bf16) for _ in SLICES),
            vmem((2, 6, 512, BLK), bf16),
            vmem((NQ // 2, 8, BLK), f32),
            tuple(ring_scratch(*rows) for rows in SLICES),
            vmem((2, SPARE // 2, 8, BLK), f32),
            vmem((NQ, 8, BLK), f32),
            vmem((NQ, 8, BLK), f32),
            dma((2, 2, 3)),
            dma((2, 2, 3)),
            dma((2, 4)),
            dma((2, 4)),
            dma((2, 8)),
            dma((2, 8)),
            dma,
            dma((4,)),
            dma((8,)),
            dma((4,)),
            dma((4, 2)),
            dma((2, 2)),
            dma((2, 2)),
        ],
        compiler_params=pltpu.CompilerParams(
            collective_id=0, has_side_effects=True, vmem_limit_bytes=58 * 1024 * 1024
        ),
    )(block_owner.reshape(1, 72), activations, cotangent, left_factor, right_factor, left_basis, right_basis)
    update, *results = hand_over(slots, returned, results)
    return (jnp.swapaxes(update, 0, 1), *results)


def solution(mesh):
    placed = (
        P("dp", "mp"),
        P("dp", "mp"),
        P(),
        P("dp", "mp", None),
        P("dp", "mp", None),
        P("dp", "mp", None),
        P("dp", "mp", None),
    )
    return jax.shard_map(
        on_device,
        mesh=mesh,
        in_specs=placed,
        out_specs=(
            P("dp", None, "mp"),
            P("dp", "mp", None),
            P("dp", "mp", None),
            P("dp", "mp", None),
            P("dp", "mp", None),
        ),
        check_vma=False,
    )
```

```python
import functools
import math

import jax
import jax.numpy as jnp
from jax import lax
from jax.experimental import pallas as pl
from jax.experimental.pallas import tpu as pltpu
from jax.sharding import PartitionSpec as P

NSTEPS = 6
BETA = 0.9
EPS = 1e-06
MESH = pl.DeviceIdType.MESH
NX, NY, NZ, NQ = 4, 4, 8, 32
BLK = 256
SLICES = ((64, 64), (96, 64))
SPARE = 8
PROWS = 128
ORDER = (
    ("gf", 0, 1),
    ("gf", 0, 0),
    ("gf", 0, 3),
    ("gf", 0, 2),
    ("gs", 1),
    ("gsh", 0),
    ("ge", 0, 1),
    ("ge", 0, 0),
    ("ge", 0, 2),
    ("ge", 0, 3),
    ("gd", 0),
    ("P", 0, 4),
    ("AY2", 0, 4, 0),
    ("B", 0, 4, 0, 0),
    ("B", 0, 4, 0, 1),
    ("AY2", 0, 4, 1),
    ("gf", 1, 1),
    ("B", 0, 4, 1, 0),
    ("B", 0, 4, 1, 1),
    ("P", 0, 2),
    ("P", 0, 5),
    ("gf", 1, 0),
    ("P", 0, 3),
    ("AY2", 0, 3, 0),
    ("gf", 1, 2),
    ("B", 0, 3, 0, 0),
    ("B", 0, 3, 0, 1),
    ("AY1", 0, 4, 1),
    ("sec", 0),
    ("gf", 1, 3),
    ("AY2", 0, 3, 1),
    ("AY1", 0, 4, 0),
    ("B", 0, 3, 1, 0),
    ("gsh", 1),
    ("P", 0, 1),
    ("AY1", 0, 3, 0),
    ("B", 0, 3, 1, 1),
    ("P", 0, 6),
    ("ge", 1, 1),
    ("ge", 1, 0),
    ("P", 0, 7),
    ("AY2", 0, 2, 1),
    ("ge", 1, 2),
    ("AYF", 0, 4),
    ("AZ", 0, 4, 1),
    ("ge", 1, 3),
    ("B", 0, 2, 1, 0),
    ("AY2", 0, 2, 0),
    ("B", 0, 2, 0, 0),
    ("AY2", 0, 1, 0),
    ("B", 0, 2, 0, 1),
    ("AY1", 0, 3, 1),
    ("gd", 1),
    ("P", 1, 4),
    ("AY2", 1, 4, 0),
    ("sec", 1),
    ("AZ", 0, 4, 0),
    ("B", 1, 4, 0, 1),
    ("B", 1, 4, 1, 1),
    ("B", 1, 4, 0, 0),
    ("P", 1, 3),
    ("B", 1, 4, 1, 0),
    ("AY2", 1, 4, 1),
    ("P", 1, 5),
    ("AY2", 1, 3, 1),
    ("P", 1, 2),
    ("B", 1, 3, 0, 1),
    ("AY1", 1, 4, 0),
    ("AY2", 0, 1, 1),
    ("B", 1, 3, 0, 0),
    ("B", 1, 3, 1, 1),
    ("AY2", 1, 3, 0),
    ("AY1", 1, 4, 1),
    ("AY1", 0, 2, 0),
    ("P", 1, 6),
    ("AY2", 1, 2, 1),
    ("AYF", 0, 3),
    ("B", 1, 3, 1, 0),
    ("B", 0, 2, 1, 1),
    ("AY1", 1, 3, 1),
    ("AY2", 1, 2, 0),
    ("AZ", 0, 3, 1),
    ("AZ", 0, 3, 0),
    ("P", 1, 1),
    ("B", 1, 2, 0, 0),
    ("AYF", 1, 4),
    ("B", 1, 2, 0, 1),
    ("AY1", 1, 3, 0),
    ("AZ", 1, 4, 0),
    ("AY1", 0, 2, 1),
    ("AY1", 0, 1, 1),
    ("B", 1, 2, 1, 1),
    ("P", 1, 7),
    ("AY2", 1, 1, 0),
    ("B", 0, 1, 1, 0),
    ("P", 1, 0),
    ("AZ", 1, 4, 1),
    ("AY2", 1, 0, 0),
    ("AY2", 1, 0, 1),
    ("B", 1, 2, 1, 0),
    ("B", 0, 1, 0, 1),
    ("AY1", 1, 2, 0),
    ("AY2", 1, 1, 1),
    ("AY1", 1, 2, 1),
    ("AY1", 0, 1, 0),
    ("B", 1, 1, 0, 0),
    ("AYF", 0, 2),
    ("AYF", 1, 3),
    ("B", 1, 1, 0, 1),
    ("P", 0, 0),
    ("B", 0, 1, 0, 0),
    ("AZ", 1, 3, 1),
    ("B", 1, 1, 1, 1),
    ("AY2", 0, 0, 1),
    ("AZ", 1, 3, 0),
    ("AY2", 0, 0, 0),
    ("AY1", 1, 1, 0),
    ("B", 1, 1, 1, 0),
    ("AY1", 1, 1, 1),
    ("AZ", 0, 2, 0),
    ("BF", 1, 0),
    ("B", 0, 1, 1, 1),
    ("AZ", 0, 2, 1),
    ("BY2", 1, 0),
    ("BY2", 1, 1),
    ("BF", 0, 0),
    ("BY2", 0, 1),
    ("BY2", 0, 0),
    ("AY1", 0, 0, 0),
    ("AY1", 0, 0, 1),
    ("AYF", 1, 2),
    ("AZ", 1, 2, 0),
    ("AZ", 1, 2, 1),
    ("AY1", 1, 0, 1),
    ("AY1", 1, 0, 0),
    ("AYF", 1, 1),
    ("BY1", 1, 1),
    ("BF", 1, 1),
    ("BY1", 1, 0),
    ("BF", 0, 1),
    ("AYF", 0, 1),
    ("BY1", 0, 1),
    ("AZ", 0, 1, 0),
    ("BY1", 0, 0),
    ("AZ", 0, 1, 1),
    ("AZ", 1, 1, 1),
    ("AZ", 1, 1, 0),
    ("FB", 1),
    ("sx", 1),
    ("AYF", 0, 0),
    ("AYF", 1, 0),
    ("FA", 0),
    ("FB", 0),
    ("sw", 1),
    ("FA", 1),
)


def place():
    dp = lax.axis_index("dp")
    x = lax.axis_index("mp")
    return x, lax.rem(lax.div(dp, 2), NY), lax.div(dp, 2 * NY), lax.rem(dp, 2)


def device(dx=0, dy=0, dz=0, dc=0):
    x, y, z, c = place()
    x = lax.rem(x + dx + NX, NX)
    y = lax.rem(y + dy + NY, NY)
    z = lax.rem(z + dz + NZ, NZ)
    c = lax.rem(c + dc, 2)
    return ((z * NY + y) * 2 + c, x)


def remote(src, dst, send, recv, target):
    return pltpu.make_async_remote_copy(
        src_ref=src, dst_ref=dst, send_sem=send, recv_sem=recv, device_id=target, device_id_type=MESH
    )


def encode(read, groups, dst):
    exponents = []
    for g in range(groups):
        value = read(g)
        top = jnp.max(jnp.abs(value), axis=0, keepdims=True)
        exponent = jnp.ceil(jnp.log2(jnp.maximum(top, 1e-30) * (1.0 / 32700.0)))
        exponents.append(exponent)
        coded = jnp.round(value * jnp.exp2(-exponent))
        dst[pl.ds(16 * g, 16), :] = coded.astype(jnp.int32).astype(jnp.int16)
    exponents.append(jnp.zeros((16 - groups, BLK), jnp.float32))
    tile = jnp.concatenate(exponents, axis=0)
    dst[pl.ds(16 * groups, 16), :] = tile.astype(jnp.int32).astype(jnp.int16)


def decoder(src, groups):
    scales = jnp.exp2(src[pl.ds(16 * groups, 16), :].astype(jnp.int32).astype(jnp.float32))

    def read(g):
        value = src[pl.ds(16 * g, 16), :].astype(jnp.int32).astype(jnp.float32)
        return value * scales[g : g + 1, :]

    return read


def split(value):
    high = value.astype(jnp.bfloat16)
    return high, (value - high.astype(jnp.float32)).astype(jnp.bfloat16)


def turned(parts):
    return parts[0].T, parts[1].T


def times(left_parts, right_parts):
    def dot(a, b):
        return jnp.dot(a, b, preferred_element_type=jnp.float32)

    both = dot(jnp.concatenate(left_parts, axis=0), right_parts[0])
    return both[:BLK] + (both[BLK:] + dot(left_parts[0], right_parts[1]))


def refresh(gradient, held, fresh, k, live):
    def keep(n, value):
        fresh[n, k] = value if live is None else jnp.where(live, value, held[n, k])

    g = split(gradient)
    gt = turned(g)
    share = (1.0 - BETA) / BLK
    factors = [BETA * held[0, k] + share * times(g, gt), BETA * held[1, k] + share * times(gt, g)]
    powers, scales = [], []
    for n in range(2):
        keep(n, factors[n])
        power = times(split(factors[n]), split(held[2 + n, k]))
        square = jnp.sum(power * power, axis=0, keepdims=True)
        scales.append(jnp.exp(-0.125 * jnp.log(square * (1.0 / BLK) + EPS)))
        powers.append(power / jnp.sqrt(jnp.sum(square, axis=1, keepdims=True) + EPS))

    def step(_, values):
        parts = [split(v) for v in values]
        grams = [times(turned(p), p) for p in parts]
        moves = [times(p, split(gram)) for p, gram in zip(parts, grams)]
        return tuple(1.5 * v - 0.5 * m for v, m in zip(values, moves))

    bases = lax.fori_loop(0, NSTEPS, step, tuple(powers))
    weights = []
    for n in range(2):
        keep(2 + n, bases[n])
        weights.append(times(split(bases[n] * scales[n]), turned(split(bases[n]))))
    inner = times(g, split(weights[1]))
    return times(split(weights[0]), split(inner))


def gradient_kernel(
    token_scale,
    owner_ref,
    act_hbm,
    cot_hbm,
    left_hbm,
    right_hbm,
    left_basis_hbm,
    right_basis_hbm,
    slots_out,
    ret_out,
    left_out,
    right_out,
    left_basis_out,
    right_basis_out,
    owner_v,
    act_ref,
    held,
    fresh,
    grad,
    u_send,
    ret,
    table_v,
    table_s,
    at,
    cot2,
    spill,
    rings,
    sec,
    sec_out,
    sec_in,
    x_send,
    x_recv,
    f_send,
    f_recv,
    c_send,
    c_recv,
    t_sem,
    s_sem,
    in_sem,
    held_sem,
    out_sem,
    u_sem,
    r_sem,
):
    x, y, z, c = place()
    me_q = z * NY + y
    other = device(dc=1)

    def act_in(n):
        columns = pl.ds(n * 384, 384)
        return pltpu.make_async_copy(act_hbm.at[:, columns], act_ref.at[:, columns], in_sem.at[6 + n])

    def cot_in(j):
        return pltpu.make_async_copy(cot_hbm.at[:, pl.ds(j * BLK, BLK)], cot2.at[0, j], in_sem.at[j])

    factors = (left_hbm, right_hbm, left_basis_hbm, right_basis_hbm)
    results = (left_out, right_out, left_basis_out, right_basis_out)

    def held_in(n):
        return pltpu.make_async_copy(factors[n], held.at[n], held_sem.at[n])

    def fresh_out(n, k):
        return pltpu.make_async_copy(fresh.at[n, k], results[n].at[k], out_sem.at[n, k])

    barrier = pltpu.get_barrier_semaphore()
    act_in(0).start()
    act_in(1).start()
    neighbours = [device(dx=1), device(dx=3), device(dy=1), device(dy=3), device(dz=1), device(dz=7), other]
    for target in neighbours:
        pl.semaphore_signal(barrier, inc=1, device_id=target, device_id_type=MESH)
    for j in range(6):
        cot_in(j).start()

    def turn(s, p):
        at[s][0, p] = act_ref[:, pl.ds(p * BLK + s * PROWS, PROWS)].T

    def own_piece(s, p, d):
        sgn = 1 - 2 * d
        return remote(
            at[s].at[0, p],
            at[s].at[0, 3 * ((4 - sgn) % 4) + p],
            x_send.at[s, d, p],
            x_recv.at[s, d, p],
            device(dx=sgn),
        )

    far = ((0, 0, 128, 0), (2, 0, 128, 1), (1, 0, 64, 0), (1, 64, 64, 1))

    def forward_piece(s, n):
        p, start, size, d = far[n]
        sgn = 1 - 2 * d
        rows = pl.ds(start, size)
        return remote(
            at[s].at[0, 3 * ((4 - sgn) % 4) + p, rows],
            at[s].at[0, 6 + p, rows],
            f_send.at[s, n],
            f_recv.at[s, n],
            device(dx=sgn),
        )

    def core_shard(s, r):
        rows = pl.ds(3 * r, 3)
        n = {0: 0, 3: 1, 1: 2}[r]
        return remote(at[s].at[0, rows], at[s].at[1, rows], c_send.at[s, n], c_recv.at[s, n], other)

    def core_piece(s, n):
        p, start, size, _ = far[n]
        rows = pl.ds(start, size)
        return remote(
            at[s].at[0, 6 + p, rows], at[s].at[1, 6 + p, rows], c_send.at[s, 3 + n], c_recv.at[s, 3 + n], other
        )

    def gather_start(s):
        for n in range(3):
            own_piece(s, n, 0).start()
            own_piece(s, 2 - n, 1).start()
        core_shard(s, 0).start()

    def forward(s, n):
        p, _, _, d = far[n]
        own_piece(s, p, d).wait_recv()
        forward_piece(s, n).start()

    def share(s):
        own_piece(s, 2, 0).wait_recv()
        own_piece(s, 0, 1).wait_recv()
        core_shard(s, 3).start()
        core_shard(s, 1).start()

    def pass_on(s, n):
        forward_piece(s, n).wait_recv()
        core_piece(s, n).start()

    def gathered(s):
        for r in (0, 3, 1):
            core_shard(s, r).wait_recv()
        for n in range(4):
            core_piece(s, n).wait_recv()
        if s == 0:
            cot_copy.wait_recv()

    act_in(0).wait()
    act_in(1).wait()
    for p in (0, 2, 1):
        turn(0, p)
    pl.semaphore_wait(barrier, 7)
    gather_start(0)
    for n in range(4):
        held_in(n).start()
    for j in range(6):
        cot_in(j).wait()
    cot_copy = remote(cot2.at[0], cot2.at[1], c_send.at[0, 7], c_recv.at[0, 7], other)
    cot_copy.start()
    for p in range(3):
        turn(1, p)

    owner_v[...] = jnp.full((1, 128), -1, jnp.int32)
    owner_v[:, pl.ds(0, 72)] = owner_ref[...]
    owners = owner_v[...]
    lanes = lax.broadcasted_iota(jnp.int32, (128, 128), 1)
    subs = lax.broadcasted_iota(jnp.int32, (128, 128), 0)
    earlier = lanes < subs
    owner_column = jnp.broadcast_to(owners, (128, 128)).T
    same = owner_column == owners
    is_second = jnp.max(jnp.where(same & earlier & (subs < 72), 1, 0), axis=1, keepdims=True)
    is_second = jnp.broadcast_to(is_second, (128, 128))
    second_row = is_second.T
    rank = jnp.sum(jnp.where(earlier, second_row, 0), axis=1, keepdims=True)
    rank = jnp.broadcast_to(rank, (128, 128))
    rank_row = rank.T
    mine = owners == subs
    first = jnp.min(jnp.where(mine, lanes, 71), axis=1, keepdims=True)
    entry = jnp.sum(jnp.where(mine, second_row * rank_row, 0), axis=1, keepdims=True)
    numbers = jnp.sum(jnp.where(rank == lanes, is_second * subs, 0), axis=0, keepdims=True)
    entry = jnp.minimum(entry, SPARE - 1)
    count = jnp.sum(jnp.where(mine, 1, 0), axis=1, keepdims=True)
    columns = jnp.where(lanes == 0, first, jnp.where(lanes == 1, entry, count))
    table_v[0:128, :] = columns
    table_v[128:136, :] = jnp.broadcast_to(numbers, (8, 128))
    slots_out[...] = (2 * owners + second_row[0:1, :])[:, 0:72]
    table_copy = pltpu.make_async_copy(table_v, table_s, t_sem)
    table_copy.start()
    table_copy.wait()

    def product_of(block, s):
        band = lax.rem(lax.div(block, 6) - 3 * x + 12, 12)
        column = lax.rem(block, 6)
        total = jnp.dot(at[s][0, band], cot2[0, column], preferred_element_type=jnp.float32)
        total += jnp.dot(at[s][1, band], cot2[1, column], preferred_element_type=jnp.float32)
        return total * token_scale

    def ring(s):
        ra, rb = SLICES[s]
        part = rings[s]["part"]
        wire = rings[s]["wire"]
        sems = rings[s]["sems"]

        def hop(name, index, target, rows=None):
            src, dst = wire[name]
            send, recv = sems[name].at[(0,) + index], sems[name].at[(1,) + index]
            if rows is not None:
                index = index + (pl.ds(0, rows),)
            return remote(src.at[index], dst.at[index], send, recv, target)

        def produce(dz):
            @pl.loop(0, NY, unroll=True)
            def _(dy):
                q = lax.rem(z + dz, NZ) * NY + lax.rem(y + dy, NY)
                part[dz, dy, pl.ds(0, PROWS), :] = product_of(table_s[2 * q + c, 0], s)

        def rows_of(dz, dy, start):
            def read(g):
                return part[dz, dy, pl.ds(start + 16 * g, 16), :]

            return read

        def joined(reads, groups):
            def read(g):
                return reads[g // groups](g % groups)

            return read

        def plus(first_read, second_read, low, high, shift=0):
            def read(g):
                if low <= g < high:
                    return first_read(g) + second_read(g - low + shift)
                return first_read(g)

            return read

        ga, gb = ra // 16, rb // 16
        pairs = {4: (4,), 3: (3, 5), 2: (2, 6), 1: (1, 7), 0: (0,)}

        def y_target(d):
            return device(dy=1 - 2 * d)

        def z_target(d):
            return device(dz=1 - 2 * d)

        def a_y2(k, d):
            rows = len(pairs[k]) * ra // 2 + 16
            reads = [rows_of(dz, 2, d * (ra // 2)) for dz in pairs[k]]
            encode(joined(reads, ga // 2), len(reads) * ga // 2, wire["ya2"][0].at[k, d])
            hop("ya2", (k, d), y_target(d), rows).start()

        def a_y1(k, d):
            count = len(pairs[k])
            hop("ya2", (k, d), y_target(d), count * ra // 2 + 16).wait_recv()
            arrived = decoder(wire["ya2"][1].at[k, d], count * ga // 2)
            low = d * (ga // 2)
            reads = [
                plus(rows_of(dz, 1 + 2 * d, 0), arrived, low, low + ga // 2, n * (ga // 2))
                for n, dz in enumerate(pairs[k])
            ]
            encode(joined(reads, ga), count * ga, wire["ya1"][0].at[k, d])
            hop("ya1", (k, d), y_target(d), count * ra + 16).start()

        def a_yf(k):
            count = len(pairs[k])
            for d in range(2):
                hop("ya1", (k, d), y_target(d), count * ra + 16).wait_recv()
            left, right = [decoder(wire["ya1"][1].at[k, d], count * ga) for d in range(2)]
            for n, dz in enumerate(pairs[k]):
                for g in range(ga):
                    part[dz, 0, pl.ds(16 * g, 16), :] += left(n * ga + g) + right(n * ga + g)

        def a_z(k, d):
            dz = k if d == 0 else 8 - k
            if k == 4:
                encode(rows_of(4, 0, d * (ra // 2)), ga // 2, wire["za4"][0].at[d])
                hop("za4", (d,), z_target(d)).start()
                return
            if k == 3:
                hop("za4", (d,), z_target(d)).wait_recv()
                low = d * (ga // 2)
                read = plus(rows_of(dz, 0, 0), decoder(wire["za4"][1].at[d], ga // 2), low, low + ga // 2)
            else:
                hop("za", (k, d), z_target(d)).wait_recv()
                read = plus(rows_of(dz, 0, 0), decoder(wire["za"][1].at[k, d], ga), 0, ga)
            encode(read, ga, wire["za"][0].at[k - 1, d])
            hop("za", (k - 1, d), z_target(d)).start()

        def b_z(k, n, d):
            dz = k if d == 0 else 8 - k
            dys = (2 - 2 * n, 3 - 2 * n)
            if k == 4:
                reads = [rows_of(4, dy, ra + d * (rb // 2)) for dy in dys]
                encode(joined(reads, gb // 2), gb, wire["zb4"][0].at[n, d])
                hop("zb4", (n, d), z_target(d)).start()
                return
            if k == 3:
                hop("zb4", (n, d), z_target(d)).wait_recv()
                arrived = decoder(wire["zb4"][1].at[n, d], gb)
                low, many = d * (gb // 2), gb // 2
            else:
                hop("zb", (k, n, d), z_target(d)).wait_recv()
                arrived = decoder(wire["zb"][1].at[k, n, d], 2 * gb)
                low, many = 0, gb
            reads = [plus(rows_of(dz, dy, ra), arrived, low, low + many, m * many) for m, dy in enumerate(dys)]
            encode(joined(reads, gb), 2 * gb, wire["zb"][0].at[k - 1, n, d])
            hop("zb", (k - 1, n, d), z_target(d)).start()

        def b_zf(n):
            for d in range(2):
                hop("zb", (0, n, d), z_target(d)).wait_recv()
            left, right = [decoder(wire["zb"][1].at[0, n, d], 2 * gb) for d in range(2)]
            for m in range(2):
                for g in range(gb):
                    part[0, 2 - 2 * n + m, pl.ds(ra + 16 * g, 16), :] += left(m * gb + g) + right(m * gb + g)

        def b_y2(d):
            encode(rows_of(0, 2, ra + d * (rb // 2)), gb // 2, wire["yb2"][0].at[d])
            hop("yb2", (d,), y_target(d)).start()

        def b_y1(d):
            hop("yb2", (d,), y_target(d)).wait_recv()
            low = d * (gb // 2)
            arrived = decoder(wire["yb2"][1].at[d], gb // 2)
            encode(plus(rows_of(0, 1 + 2 * d, ra), arrived, low, low + gb // 2), gb, wire["yb1"][0].at[d])
            hop("yb1", (d,), y_target(d)).start()

        def finish_b():
            for d in range(2):
                hop("yb1", (d,), y_target(d)).wait_recv()
            left, right = [decoder(wire["yb1"][1].at[d], gb) for d in range(2)]
            for g in range(gb):
                store_b(s, g, part[0, 0, pl.ds(ra + 16 * g, 16), :] + left(g) + right(g))

        def finish_a():
            for d in range(2):
                hop("za", (0, d), z_target(d)).wait_recv()
            left, right = [decoder(wire["za"][1].at[0, d], ga) for d in range(2)]
            for g in range(ga):
                grad[0, pl.ds(PROWS * s + 16 * g, 16), :] = part[0, 0, pl.ds(16 * g, 16), :] + left(g) + right(g)

        def drain():
            for d in range(2):
                for k in range(5):
                    hop("ya2", (k, d), y_target(d), len(pairs[k]) * ra // 2 + 16).wait_send()
                    hop("ya1", (k, d), y_target(d), len(pairs[k]) * ra + 16).wait_send()
                hop("za4", (d,), z_target(d)).wait_send()
                hop("yb2", (d,), y_target(d)).wait_send()
                hop("yb1", (d,), y_target(d)).wait_send()
                for k in range(3):
                    hop("za", (k, d), z_target(d)).wait_send()
                    for n in range(2):
                        hop("zb", (k, n, d), z_target(d)).wait_send()
                for n in range(2):
                    hop("zb4", (n, d), z_target(d)).wait_send()

        return {
            "P": produce,
            "AY2": a_y2,
            "AY1": a_y1,
            "AYF": a_yf,
            "AZ": a_z,
            "B": b_z,
            "BF": b_zf,
            "BY2": b_y2,
            "BY1": b_y1,
            "FB": finish_b,
            "FA": finish_a,
            "drain": drain,
        }

    def store_b(s, g, rows):
        if s == 0 or g < 2:
            grad[0, pl.ds(PROWS * s + SLICES[s][0] + 16 * g, 16), :] = rows
        else:
            sec[c, pl.ds(2 * (g - 2), 2)] = rows.reshape(2, 8, BLK)

    def second_rows(h):
        ra = SLICES[1][0]

        @pl.loop(0, SPARE // 2, unroll=2)
        def _(s):
            spill[...] = product_of(table_s[128, 2 * s + c], h).reshape(NQ // 2, 8, BLK)

            @pl.loop(0, NQ // 2, unroll=True)
            def _(r):
                q = r + h * (NQ // 2)
                dz = lax.rem(lax.div(q, NY) - z + NZ, NZ)
                dy = lax.rem(lax.rem(q, NY) - y + NY, NY)
                rings[1]["part"][dz, dy, pl.ds(pl.multiple_of(PROWS + 8 * s, 8), 8), :] = spill[r]

    sec_copy = remote(sec.at[c], sec.at[c], s_sem.at[0], s_sem.at[1], other)

    def second_share(_):
        sec_copy.start()

    def second_send(_):
        sec_copy.wait_recv()

        @pl.loop(0, NQ, unroll=True)
        def _(q):
            place_of = table_s[2 * q + c, 1]
            sec_out[q] = sec[lax.rem(place_of, 2), lax.div(place_of, 2)]

        @pl.loop(1, NQ, unroll=True)
        def _(r):
            q = lax.rem(me_q + r, NQ)
            remote(sec_out.at[q], sec_in.at[me_q], s_sem.at[2], s_sem.at[3], (q * 2 + c, x)).start()

    tasks = [ring(0), ring(1)]
    gather = {
        "gs": gather_start,
        "gf": forward,
        "gsh": share,
        "ge": pass_on,
        "gd": gathered,
        "sec": second_rows,
        "sx": second_share,
        "sw": second_send,
    }
    for name, s, *rest in ORDER:
        (gather[name] if name in gather else tasks[s][name])(*(([s] if name in gather else []) + rest))
    whole = remote(sec_out.at[pl.ds(0, NQ - 1)], sec_in.at[pl.ds(0, NQ - 1)], s_sem.at[2], s_sem.at[3], other)
    for n in range(4):
        held_in(n).wait()

    def u_whole(k):
        part_of = pl.ds(0, NQ - 1)
        return remote(u_send.at[k, part_of], ret.at[k, c, part_of], u_sem.at[0, k], u_sem.at[1, k], other)

    def u_core(k):
        return remote(ret.at[k, c], ret.at[k, c], r_sem.at[0, k], r_sem.at[1, k], other)

    def finish(k):
        update = refresh(grad[k], held, fresh, k, None if k == 0 else table_s[me_q * 2 + c, 2] > 1)
        for n in range(4):
            fresh_out(n, k).start()
        rows = update.reshape(NQ, 8, BLK)
        halves = jnp.concatenate([rows[:, :, : BLK // 2], rows[:, :, BLK // 2 :]], axis=1)
        u_send[k] = halves.astype(jnp.bfloat16)

        @pl.loop(1, NQ, unroll=True)
        def _(r):
            q = lax.rem(me_q + r, NQ)
            remote(u_send.at[k, q], ret.at[k, c, me_q], u_sem.at[0, k], u_sem.at[1, k], (q * 2 + c, x)).start()

        ret[k, c, me_q] = u_send[k, me_q]

    finish(0)
    whole.wait_recv()
    sec_in[me_q] = sec_out[me_q]
    grad[1] = sec_in[...].reshape(BLK, BLK)
    finish(1)
    for k in range(2):
        u_whole(k).wait_recv()
        u_core(k).start()
    for k in range(2):
        u_core(k).wait_recv()

    ret_copy = pltpu.make_async_copy(ret, ret_out, t_sem)
    ret_copy.start()
    for k in range(2):
        u_whole(k).wait_send()
        u_core(k).wait_send()
        for n in range(4):
            fresh_out(n, k).wait()

    whole.wait_send()
    sec_copy.wait_send()
    cot_copy.wait_send()
    for s in range(2):
        for r in (0, 3, 1):
            core_shard(s, r).wait_send()
        for n in range(4):
            core_piece(s, n).wait_send()
            forward_piece(s, n).wait_send()
        for p in range(3):
            own_piece(s, p, 0).wait_send()
            own_piece(s, p, 1).wait_send()
    tasks[0]["drain"]()
    tasks[1]["drain"]()
    ret_copy.wait()


def hand_over(slots, returned, results):
    def body(slot_ref, ret_hbm, *refs):
        sources, update_ref, targets = refs[:4], refs[4], refs[5:9]
        ret, held, in_sem, out_sem = refs[9:]
        core = lax.rem(lax.axis_index("dp"), 2)
        loads = [pltpu.make_async_copy(sources[n], held.at[n], in_sem.at[n]) for n in range(4)]
        stores = [pltpu.make_async_copy(held.at[n], targets[n], out_sem.at[n]) for n in range(4)]
        rows_in = pltpu.make_async_copy(ret_hbm, ret, in_sem.at[4])
        rows_in.start()
        for load in loads:
            load.start()
        for load, store in zip(loads, stores):
            load.wait()
            store.start()
        rows_in.wait()
        for i in range(12):
            for j in range(6):
                slot = slot_ref[0, 6 * i + j]
                tile = ret[lax.rem(slot, 2), lax.rem(lax.div(slot, 2), 2), lax.div(slot, 4)].astype(jnp.float32)
                for h in range(2):
                    rows = jnp.where(core == 0, tile[8 * h : 8 * h + 4], tile[8 * h + 4 : 8 * h + 8])
                    columns = pl.ds(j * BLK + h * (BLK // 2), BLK // 2)
                    update_ref[i, :, columns] = rows.astype(jnp.bfloat16)
        for store in stores:
            store.wait()

    anywhere = pl.BlockSpec(memory_space=pl.ANY)
    return pl.pallas_call(
        body,
        out_shape=(jax.ShapeDtypeStruct((12, 4, 1536), jnp.bfloat16),)
        + tuple(jax.ShapeDtypeStruct(r.shape, r.dtype) for r in results),
        in_specs=[pl.BlockSpec(memory_space=pltpu.SMEM)] + [anywhere] * 5,
        out_specs=[pl.BlockSpec(memory_space=pltpu.VMEM)] + [anywhere] * 4,
        scratch_shapes=[
            pltpu.VMEM(returned.shape, returned.dtype),
            pltpu.VMEM((4, 2, BLK, BLK), jnp.float32),
            pltpu.SemaphoreType.DMA((5,)),
            pltpu.SemaphoreType.DMA((4,)),
        ],
    )(slots, returned, *results)


def on_device(
    activations, cotangent, block_owner, left_factor, right_factor, left_basis, right_basis
):
    token_scale = 1.0 / math.sqrt(activations.shape[0] * lax.axis_size("dp"))
    i16, f32, i32, bf16 = jnp.int16, jnp.float32, jnp.int32, jnp.bfloat16
    vmem, dma = pltpu.VMEM, pltpu.SemaphoreType.DMA

    def pair(*shape):
        return (vmem(shape + (BLK,), i16), vmem(shape + (BLK,), i16))

    def ring_scratch(ra, rb):
        return dict(
            part=vmem((NZ, NY, ra + rb, BLK), f32),
            wire=dict(
                ya2=pair(5, 2, ra + 16),
                ya1=pair(5, 2, 2 * ra + 16),
                za4=pair(2, ra // 2 + 16),
                za=pair(3, 2, ra + 16),
                zb4=pair(2, 2, rb + 16),
                zb=pair(3, 2, 2, 2 * rb + 16),
                yb2=pair(2, rb // 2 + 16),
                yb1=pair(2, rb + 16),
            ),
            sems=dict(
                ya2=dma((2, 5, 2)),
                ya1=dma((2, 5, 2)),
                za4=dma((2, 2)),
                za=dma((2, 3, 2)),
                zb4=dma((2, 2, 2)),
                zb=dma((2, 3, 2, 2)),
                yb2=dma((2, 2)),
                yb1=dma((2, 2)),
            ),
        )

    whole = pl.BlockSpec(memory_space=pltpu.VMEM)
    anywhere = pl.BlockSpec(memory_space=pl.ANY)
    slots, returned, *results = pl.pallas_call(
        functools.partial(gradient_kernel, token_scale),
        out_shape=(jax.ShapeDtypeStruct((1, 72), i32), jax.ShapeDtypeStruct((2, 2, NQ, 16, BLK // 2), bf16))
        + tuple(jax.ShapeDtypeStruct((2, BLK, BLK), f32) for _ in range(4)),
        in_specs=[whole] + [anywhere] * 6,
        out_specs=[whole] + [anywhere] * 5,
        scratch_shapes=[
            vmem((1, 128), i32),
            vmem((512, 768), bf16),
            vmem((4, 2, BLK, BLK), f32),
            vmem((4, 2, BLK, BLK), f32),
            vmem((2, BLK, BLK), f32),
            vmem((2, NQ, 16, BLK // 2), bf16),
            vmem((2, 2, NQ, 16, BLK // 2), bf16),
            vmem((136, 128), i32),
            pltpu.SMEM((136, 128), i32),
            tuple(vmem((2, 3 * NX, PROWS, 512), bf16) for _ in SLICES),
            vmem((2, 6, 512, BLK), bf16),
            vmem((NQ // 2, 8, BLK), f32),
            tuple(ring_scratch(*rows) for rows in SLICES),
            vmem((2, SPARE // 2, 8, BLK), f32),
            vmem((NQ, 8, BLK), f32),
            vmem((NQ, 8, BLK), f32),
            dma((2, 2, 3)),
            dma((2, 2, 3)),
            dma((2, 4)),
            dma((2, 4)),
            dma((2, 8)),
            dma((2, 8)),
            dma,
            dma((4,)),
            dma((8,)),
            dma((4,)),
            dma((4, 2)),
            dma((2, 2)),
            dma((2, 2)),
        ],
        compiler_params=pltpu.CompilerParams(
            collective_id=0, has_side_effects=True, vmem_limit_bytes=58 * 1024 * 1024
        ),
    )(block_owner.reshape(1, 72), activations, cotangent, left_factor, right_factor, left_basis, right_basis)
    update, *results = hand_over(slots, returned, results)
    return (jnp.swapaxes(update, 0, 1), *results)


def solution(mesh):
    placed = (
        P("dp", "mp"),
        P("dp", "mp"),
        P(),
        P("dp", "mp", None),
        P("dp", "mp", None),
        P("dp", "mp", None),
        P("dp", "mp", None),
    )
    return jax.shard_map(
        on_device,
        mesh=mesh,
        in_specs=placed,
        out_specs=(
            P("dp", None, "mp"),
            P("dp", "mp", None),
            P("dp", "mp", None),
            P("dp", "mp", None),
            P("dp", "mp", None),
        ),
        check_vma=False,
    )
```
